32 devices in a mesh: dp: 4 (over z), expert: 8 (over y, x, core).
Axes of the slice: x: 2, y: 2, z: 4, core: 2. Of those that a mesh axis runs over, the one named last changes fastest.
Arguments:
- inputs: bfloat16 [8, 576, 384], P('dp', 'expert'), may hold values from -6 to 6
- attention_routes: int32 [2, 8, 576, 4], P(None, 'dp', 'expert'), may hold values from 0 to 7, all different within a row; in each aligned block of 72 rows (0 to 71, 72 to 143, ..., all dimensions but the last counted through in order) at most 48 rows name the same one
- perceptron_routes: int32 [2, 8, 576, 4], P(None, 'dp', 'expert'), may hold values from 0 to 7, all different within a row; in each aligned block of 72 rows (0 to 71, 72 to 143, ..., all dimensions but the last counted through in order) at most 48 rows name the same one
- task_index: int32 [8], P('dp'), may hold values from 0 to 12
- attention_gain: float32 [2, 384], replicated, may hold values from 0.5 to 1.5
- attention_shift: float32 [2, 384], replicated, may hold values from -1.2 to 1.2
- perceptron_gain: float32 [2, 384], replicated, may hold values from 0.5 to 1.5
- perceptron_shift: float32 [2, 384], replicated, may hold values from -1.2 to 1.2
- key_weight: bfloat16 [2, 384, 384], replicated, may hold values from -0.3125 to 0.3125
- value_weight: bfloat16 [2, 384, 384], replicated, may hold values from -0.3125 to 0.3125
- query_weight: bfloat16 [2, 8, 384, 384], P(None, 'expert'), may hold values from -0.3125 to 0.3125
- output_weight: bfloat16 [2, 8, 384, 384], P(None, 'expert'), may hold values from -4 to 4
- up_weight: bfloat16 [2, 8, 384, 1536], P(None, 'expert'), may hold values from -0.3125 to 0.3125
- down_weight: bfloat16 [2, 8, 1536, 384], P(None, 'expert'), may hold values from -0.4375 to 0.4375
- attention_router: bfloat16 [2, 13, 384, 8], replicated, may hold values from -0.15625 to 0.15625
- perceptron_router: bfloat16 [2, 13, 384, 8], replicated, may hold values from -0.15625 to 0.15625
- cotangent: bfloat16 [8, 576, 384], P('dp', 'expert'), may hold values from -6 to 6
Outputs:
- output: float32 [8, 576, 384], P('dp', 'expert')
- input_gradient: float32 [8, 576, 384], P('dp', 'expert')
- attention_gain_gradient: float32 [2, 384], replicated
- attention_shift_gradient: float32 [2, 384], replicated
- perceptron_gain_gradient: float32 [2, 384], replicated
- perceptron_shift_gradient: float32 [2, 384], replicated
- key_gradient: float32 [2, 384, 384], replicated
- value_gradient: float32 [2, 384, 384], replicated
- query_gradient: float32 [2, 8, 384, 384], P(None, 'expert')
- output_gradient: float32 [2, 8, 384, 384], P(None, 'expert')
- up_gradient: float32 [2, 8, 384, 1536], P(None, 'expert')
- down_gradient: float32 [2, 8, 1536, 384], P(None, 'expert')
- attention_router_gradient: float32 [2, 13, 384, 8], replicated
- perceptron_router_gradient: float32 [2, 13, 384, 8], replicated
The draws below stay inside these ranges and needn't reach their ends.
Inputs may be any that keep to these rules, and one draw needn't show every extreme that they name: `attention_routes`: each row names 4 different experts; within the rows of one device of one image (aligned blocks of 72 rows) no expert is named by more than 48 rows. `perceptron_routes`: each row names 4 different experts; within the rows of one device of one image (aligned blocks of 72 rows) no expert is named by more than 48 rows.
All inputs are finite; a program needn't handle non-finite values.
Results may differ from the reference program's by a relative error of at most 0.024.
Values may be sent and summed in bfloat16 or wider, within the bound.
No kernel may reach another device: no remote copies, remote signals or barrier semaphores. Data moves between devices by JAX's collectives and lax.ppermute only.
A program may use at most 192 MiB of HBM per device.

```python
import math
import jax
import jax.numpy as jnp
import numpy as np
from jax import lax

D = 384
HEADS = 6
FF = 1536
TASKS = 13
PATCHES = 576
LAYERS = 2
TOPK = 4
IMAGES = 8
ROWS = 72
EXPERTS = 8
CAP = 48
N_EXPERT = 8


def place_ends(array, own_key, smallest, top_value):
    dims = array.shape
    spot = [jax.random.randint(jax.random.fold_in(own_key, axis), (), 0, dims[axis]) for axis in range(len(dims))]
    array = array.at[tuple(spot)].set(smallest)
    longest = dims.index(max(dims))
    spot[longest] = (spot[longest] + 1) % dims[longest]
    return array.at[tuple(spot)].set(top_value)


def steps_of(key, extent, split, smallest, top_value):
    def one(axis_at, parts):
        draws = jax.random.uniform(jax.random.fold_in(jax.random.fold_in(key, 6), axis_at), (parts,), jnp.float32, smallest / len(split), top_value / len(split))
        return jnp.repeat(jnp.exp(draws), extent[axis_at] // parts).reshape((-1,) + (1,) * (len(extent) - axis_at - 1))

    factor_of = one(*split[0])
    for cut in split[1:]:
        factor_of = factor_of * one(*cut)
    return factor_of


def assign_block(own_key, own, number, rows, amount, top, reach, lean):
    ranking = jax.random.permutation(own_key, amount)
    heavy_load, common = portions_of(amount, rows * top, reach, lean, True), portions_of(amount, rows * top, reach, lean, False)
    places = jnp.arange(amount)

    def named(lengths, offset_by):
        used = int((lengths > 0).sum())
        fixed = max(1, used // 4)
        shifted = fixed + (places - fixed + offset_by * (used - fixed)) % max(1, amount - fixed)
        return jnp.zeros((amount,), jnp.int32).at[ranking[jnp.where(places < fixed, places, shifted)]].set(jnp.asarray(lengths, jnp.int32))

    lengths = jnp.where(number % 4 == 0, named(heavy_load, number // 4), named(common, number - number // 4 - 1))
    mixed = jax.random.permutation(jax.random.fold_in(own, 3), amount)
    donor, sink = mixed[0:amount // 2 * 2:2], mixed[1:amount // 2 * 2:2]
    room = jnp.minimum(lengths[donor] - 1, reach - lengths[sink]) // 2
    room = jnp.where((donor == ranking[0]) | (sink == ranking[0]) | (lengths[sink] == 0), 0, jnp.maximum(room, 0))
    shifted = jax.random.randint(jax.random.fold_in(own, 4), (amount // 2,), 0, 1 << 20) % (room + 1)
    lengths = lengths.at[donor].add(-shifted).at[sink].add(shifted)
    items = jnp.searchsorted(jnp.cumsum(lengths), jnp.arange(rows * top), side="right").astype(jnp.int32)
    table = items.reshape(top, rows).T
    table = table[jax.random.permutation(jax.random.fold_in(own, 1), rows)]
    offset_by = jax.random.randint(jax.random.fold_in(own, 2), (rows, 1), 0, top)
    return jnp.take_along_axis(table, (jnp.arange(top)[None, :] + offset_by) % top, axis=1)


def portions_of(amount, total, most, lean, full):
    weights = [(1 << 20) // math.isqrt(standing ** lean) + 1 for standing in range(1, amount + 1)]
    largest = most if full else min(most, max(-(-total // amount), total * weights[0] // sum(weights)))
    least = 1 if total - largest >= amount - 1 else 0
    given, surplus = [largest] + [least] * (amount - 1), total - largest - least * (amount - 1)
    while surplus > 0:
        candidates = [i for i in range(1, amount) if given[i] < largest] or [i for i in range(1, amount) if given[i] < most]
        whole, budget = sum([weights[i] for i in candidates]), surplus
        for i in candidates:
            extra = min(most - given[i], max(1, budget * weights[i] // whole), surplus)
            given[i] = given[i] + extra
            surplus = surplus - extra
    return np.array(given)


def gaussian(own_key, extent, width, limit, pieces=(), held_as=jnp.bfloat16):
    loudness = steps_of(own_key, extent, pieces, -0.22, 0.18) if pieces else 1.0
    drawn = jax.random.normal(own_key, extent, jnp.float32) * width * loudness
    return jnp.minimum(jnp.maximum(drawn, -limit), limit).astype(held_as)


def setup_inputs(seed: int = 0) -> dict:
    splits = jax.random.split(jax.random.key(seed), 18)
    inputs = gaussian(splits[0], (IMAGES, PATCHES, D), 1.0, 6.0, ((0, 4), (1, 8)))
    attention_routes_keys = jax.random.split(jax.random.fold_in(splits[1], 1), LAYERS * IMAGES * PATCHES // ROWS)
    attention_routes_turns = jax.random.permutation(jax.random.fold_in(splits[1], 3), LAYERS * IMAGES * PATCHES // ROWS)
    attention_routes = jax.vmap(lambda own, number: assign_block(jax.random.fold_in(splits[1], 2), own, number, ROWS, EXPERTS, TOPK, CAP, 1))(attention_routes_keys, attention_routes_turns).reshape((LAYERS, IMAGES, PATCHES, TOPK))
    perceptron_routes_keys = jax.random.split(jax.random.fold_in(splits[2], 1), LAYERS * IMAGES * PATCHES // ROWS)
    perceptron_routes_turns = jax.random.permutation(jax.random.fold_in(splits[2], 3), LAYERS * IMAGES * PATCHES // ROWS)
    perceptron_routes = jax.vmap(lambda own, number: assign_block(jax.random.fold_in(splits[2], 2), own, number, ROWS, EXPERTS, TOPK, CAP, 1))(perceptron_routes_keys, perceptron_routes_turns).reshape((LAYERS, IMAGES, PATCHES, TOPK))
    task_index = place_ends(jax.random.randint(splits[3], (IMAGES,), 0, TASKS), jax.random.fold_in(splits[3], 1), 0, TASKS - 1).astype(jnp.int32)
    attention_gain = jnp.clip(1.0 + 0.1 * jax.random.normal(splits[4], (LAYERS, D), jnp.float32), 0.5, 1.5)
    attention_shift = gaussian(splits[5], (LAYERS, D), 0.2, 1.2, (), jnp.float32)
    perceptron_gain = jnp.clip(1.0 + 0.1 * jax.random.normal(splits[6], (LAYERS, D), jnp.float32), 0.5, 1.5)
    perceptron_shift = gaussian(splits[7], (LAYERS, D), 0.2, 1.2, (), jnp.float32)
    key_weight = gaussian(splits[8], (LAYERS, D, D), D ** -0.5, 0.3125)
    value_weight = gaussian(splits[9], (LAYERS, D, D), D ** -0.5, 0.3125)
    query_weight = gaussian(splits[10], (LAYERS, EXPERTS, D, D), D ** -0.5, 0.3125, ((1, 8),))
    output_weight = gaussian(splits[11], (LAYERS, EXPERTS, D, D), 2 ** -0.5, 4.0, ((1, 8),))
    up_weight = gaussian(splits[12], (LAYERS, EXPERTS, D, FF), D ** -0.5, 0.3125, ((1, 8),))
    down_weight = gaussian(splits[13], (LAYERS, EXPERTS, FF, D), (FF // 8) ** -0.5, 0.4375, ((1, 8),))
    attention_router = gaussian(splits[14], (LAYERS, TASKS, D, EXPERTS), (4 * D) ** -0.5, 0.15625)
    perceptron_router = gaussian(splits[15], (LAYERS, TASKS, D, EXPERTS), (4 * D) ** -0.5, 0.15625)
    cotangent = gaussian(splits[16], (IMAGES, PATCHES, D), 1.0, 6.0, ((0, 4), (1, 8)))
    return {"inputs": inputs, "attention_routes": attention_routes, "perceptron_routes": perceptron_routes, "task_index": task_index, "attention_gain": attention_gain, "attention_shift": attention_shift, "perceptron_gain": perceptron_gain, "perceptron_shift": perceptron_shift, "key_weight": key_weight, "value_weight": value_weight, "query_weight": query_weight, "output_weight": output_weight, "up_weight": up_weight, "down_weight": down_weight, "attention_router": attention_router, "perceptron_router": perceptron_router, "cotangent": cotangent}


@jax.custom_vjp
def low(v):
    return lax.optimization_barrier(v.astype(jnp.bfloat16)).astype(jnp.float32)

@jax.custom_vjp
def low_back(v):
    return v

def low_keep(v):
    return (low(v), None)

def low_pass(kept, grad):
    return (grad,)

def back_keep(v):
    return (v, None)

def back_low(kept, grad):
    return (low(grad),)
low.defvjp(low_keep, low_pass)
low_back.defvjp(back_keep, back_low)
epsilon = 1e-06
highest = lax.Precision.HIGHEST

def layer_norm(state, gain, shift):
    centered = state - lax.optimization_barrier(jnp.mean(state, axis=-1, keepdims=True))
    variance = lax.optimization_barrier(jnp.mean(centered * centered, axis=-1, keepdims=True))
    return centered * lax.rsqrt(variance + epsilon) * gain + shift

def slot_table(routes, experts, capacity):
    picked = (routes[..., None] == jnp.arange(experts, dtype=jnp.int32)).astype(jnp.int32)
    leading = picked.shape[:-3]
    flat_pick = picked.reshape(leading + (picked.shape[-3] * picked.shape[-2], experts))
    earlier = (jnp.cumsum(flat_pick, axis=-2) - flat_pick).astype(jnp.int32)
    position = lax.optimization_barrier(jnp.sum(earlier * flat_pick, axis=-1)).astype(jnp.int32)
    return (routes.reshape(position.shape) * capacity + position).astype(jnp.int32)

def route_setup(normed_low, routes, router, experts, capacity):
    patch_count, top_count = routes.shape
    blocks = N_EXPERT
    block_rows = patch_count // blocks
    logits = jnp.dot(normed_low, router, precision=highest)
    chosen = jnp.take_along_axis(logits, routes, axis=1)
    gate_values = jax.nn.softmax(chosen, axis=-1)
    slot_index = slot_table(routes.reshape(blocks, block_rows, top_count), experts, capacity)
    slot_match = (slot_index[:, None, :] == jnp.arange(experts * capacity, dtype=jnp.int32)[None, :, None]).astype(jnp.float32)
    dispatch = lax.optimization_barrier(jnp.sum(slot_match.reshape(blocks, experts * capacity, block_rows, top_count), axis=-1))
    copies = low_back(jnp.einsum('bsr,brd->bsd', dispatch, normed_low.reshape(blocks, block_rows, -1), precision=highest))
    per_expert = copies.reshape(blocks, experts, capacity, -1).transpose(1, 0, 2, 3).reshape(experts, blocks * capacity, -1)
    return (gate_values, slot_index, per_expert)

def combine(expert_result, gate_values, slot_index, experts, capacity):
    blocks = slot_index.shape[0]
    feature_count = expert_result.shape[-1]
    by_block = expert_result.reshape(experts, blocks, capacity, feature_count).transpose(1, 0, 2, 3)
    by_block = by_block.reshape(blocks, experts * capacity, feature_count)
    picked = by_block[jnp.arange(blocks, dtype=jnp.int32)[:, None], slot_index]
    picked = picked.reshape(gate_values.shape + (feature_count,))
    return lax.optimization_barrier(jnp.sum(gate_values[..., None] * picked, axis=1))

def one_layer(state, routes_attention, routes_perceptron, layer_weights, image_task, experts, capacity):
    attention_gain, attention_shift, perceptron_gain, perceptron_shift, key_weight, value_weight, query_weight, output_weight, up_weight, down_weight, attention_router, perceptron_router = layer_weights
    head_size = D // HEADS
    score_scale = head_size ** (-0.5)
    normed_low = low(layer_norm(state, attention_gain, attention_shift))
    key_rows = low(jnp.dot(normed_low, key_weight, precision=highest))
    value_rows = low(jnp.dot(normed_low, value_weight, precision=highest))
    gate_values, slot_index, per_expert = route_setup(normed_low, routes_attention, attention_router[image_task], experts, capacity)
    queries = low_back(low(jnp.einsum('emd,edf->emf', per_expert, query_weight, precision=highest)))
    query_heads = queries.reshape(experts, -1, HEADS, head_size)
    key_heads = key_rows.reshape(-1, HEADS, head_size)
    value_heads = value_rows.reshape(-1, HEADS, head_size)
    scores = low_back(jnp.einsum('emhc,phc->ehmp', query_heads, key_heads, precision=highest) * score_scale)
    probability = low(jax.nn.softmax(scores, axis=-1))
    mixed_heads = low_back(low(jnp.einsum('ehmp,phc->emhc', probability, value_heads, precision=highest)))
    attention_result = low_back(low(jnp.einsum('emf,efd->emd', mixed_heads.reshape(experts, -1, D), output_weight, precision=highest)))
    middle = state + combine(attention_result, gate_values, slot_index, experts, capacity)
    normed_mid = low(layer_norm(middle, perceptron_gain, perceptron_shift))
    gate_mid, slot_mid, per_expert_mid = route_setup(normed_mid, routes_perceptron, perceptron_router[image_task], experts, capacity)
    hidden = low_back(jnp.einsum('emd,edf->emf', per_expert_mid, up_weight, precision=highest))
    active = low(jax.nn.gelu(hidden, approximate=False))
    perceptron_result = low_back(low(jnp.einsum('emf,efd->emd', active, down_weight, precision=highest)))
    return middle + combine(perceptron_result, gate_mid, slot_mid, experts, capacity)

def reference(inputs, attention_routes, perceptron_routes, task_index, attention_gain, attention_shift, perceptron_gain, perceptron_shift, key_weight, value_weight, query_weight, output_weight, up_weight, down_weight, attention_router, perceptron_router, cotangent):
    experts = N_EXPERT
    capacity = CAP
    weights = tuple((array_item.astype(jnp.float32) for array_item in (attention_gain, attention_shift, perceptron_gain, perceptron_shift, key_weight, value_weight, query_weight, output_weight, up_weight, down_weight, attention_router, perceptron_router)))
    routes_first = jnp.transpose(attention_routes, (1, 0, 2, 3))
    routes_second = jnp.transpose(perceptron_routes, (1, 0, 2, 3))

    def forward(state_all, weight_set):

        def per_image(items):
            state, routes_a, routes_p, image_task = items
            for layer_index in range(LAYERS):
                layer_weights = tuple((array_item[layer_index] for array_item in weight_set))
                state = one_layer(state, routes_a[layer_index], routes_p[layer_index], layer_weights, image_task, experts, capacity)
            return state
        return lax.map(jax.checkpoint(per_image), (state_all, routes_first, routes_second, task_index))
    output, pullback = jax.vjp(forward, inputs.astype(jnp.float32), weights)
    input_gradient, grads = pullback(cotangent.astype(jnp.float32))
    return (output, input_gradient, grads[0], grads[1], grads[2], grads[3], grads[4], grads[5], grads[6], grads[7], grads[8], grads[9], grads[10], grads[11])
```

```python
from functools import partial

import jax
import jax.numpy as jnp
from jax import lax
from jax.experimental import pallas as pl
from jax.experimental.pallas import tpu as pltpu
from jax.sharding import PartitionSpec as P

HEADS = 6
epsilon = 1e-06
f32, bf16 = jnp.float32, jnp.bfloat16
NN, NT, TN = ((1,), (0,)), ((1,), (1,)), ((0,), (0,))
MIB = 1 << 20


def mm(left, right, dims=NN, precision=None):
    return lax.dot_general(
        left, right, (dims, ((), ())), preferred_element_type=f32, precision=precision
    )


def whole(array):
    rank = len(array.shape)
    return pl.BlockSpec(array.shape, lambda i: (0,) * rank)


def per_image(array):
    rank = len(array.shape)
    return pl.BlockSpec((1,) + tuple(array.shape[1:]), lambda i: (i,) + (0,) * (rank - 1))


def per_image_second(array):
    rank = len(array.shape)
    return pl.BlockSpec(
        (array.shape[0], 1) + tuple(array.shape[2:]), lambda i: (0, i) + (0,) * (rank - 2)
    )


def run(name, kernel, images, ins, outs, flops, limit):
    shapes = [jax.ShapeDtypeStruct(shape, dtype) for shape, dtype, _ in outs]
    moved = sum(a.size * a.dtype.itemsize for a, _ in ins)
    moved += sum(s.size * s.dtype.itemsize for s in shapes)
    return pl.pallas_call(
        kernel,
        grid=(images,),
        in_specs=[maker(a) for a, maker in ins],
        out_specs=[maker(s) for s, (_, _, maker) in zip(shapes, outs)],
        out_shape=shapes,
        compiler_params=pltpu.CompilerParams(
            dimension_semantics=("arbitrary",), vmem_limit_bytes=limit * MIB
        ),
        cost_estimate=pl.CostEstimate(flops=flops, bytes_accessed=moved, transcendentals=0),
        name=name,
    )(*[a for a, _ in ins])


def rows_of(refs):
    return jnp.concatenate([r[0].astype(f32) for r in refs], axis=0)


def put_rows(rows, own_ref, sib_ref):
    half = own_ref.shape[0]
    size = own_ref.shape[2]
    for d in range(2 * half):
        target = own_ref if d % 2 == 0 else sib_ref
        target[d // 2, 0] = rows[d * size : (d + 1) * size].astype(bf16)


def one_hot(slot_ref, slots):
    slot = slot_ref[0]
    spots = lax.broadcasted_iota(jnp.int32, (slots, slot.shape[1]), 0)
    return spots == slot


def masked_softmax(logits, mask, axis):
    top = jnp.max(jnp.where(mask, logits, -3e38), axis=axis, keepdims=True)
    weights = jnp.where(mask, jnp.exp(jnp.minimum(logits - top, 0.0)), 0.0)
    return weights / jnp.sum(weights, axis=axis, keepdims=True)


def own_gate(rows_low, router, mask8, mine):
    gates = masked_softmax(mm(router, rows_low, NT), mask8 > 0.5, 0)
    return jnp.sum(gates * mine, axis=0, keepdims=True)


def attend_kernel(n, *refs):
    x_refs, refs = refs[:n], refs[n:]
    mask_ref, slot_ref, router_ref, mine_ref, wk, wv, wq, wo, *refs = refs
    own, sib, x_out, c_out, q_out, k_out, v_out, p_out, mixed_out, result_out, gate_out = refs
    slots, features = c_out.shape[1:]
    size = features // HEADS
    x = rows_of(x_refs).astype(bf16)
    x_out[0] = x
    hot = one_hot(slot_ref, slots)
    hot_low = hot.astype(f32).astype(bf16)
    gate_row = own_gate(x, router_ref[0], mask_ref[0], mine_ref[...])
    gate = jnp.sum(jnp.where(hot, gate_row, 0.0), axis=1, keepdims=True)
    gate_out[0] = gate
    copies = mm(hot_low, x).astype(bf16)
    c_out[0] = copies
    queries = (mm(copies, wq[...]).astype(bf16).astype(f32) * size ** (-0.5)).astype(bf16)
    q_out[0] = queries
    keys = mm(x, wk[...]).astype(bf16)
    k_out[0] = keys
    values = mm(x, wv[...])
    v_out[0] = values.astype(bf16)
    values_t = values.T.astype(bf16)
    low = lax.broadcasted_iota(jnp.int32, (slots, 2 * size), 1) < size
    zero = jnp.zeros((slots, 2 * size), bf16)
    mixed_t = []
    for head in range(HEADS):
        lanes = slice(head // 2 * 2 * size, (head // 2 + 1) * 2 * size)
        q_head = jnp.where(low if head % 2 == 0 else jnp.logical_not(low), queries[:, lanes], zero)
        scores = mm(keys[:, lanes], q_head, NT)
        weights = jnp.exp(scores - jnp.max(scores, axis=0, keepdims=True))
        inverse = 1.0 / jnp.sum(weights, axis=0, keepdims=True)
        probs = (weights * inverse).astype(bf16)
        p_out[0, head] = probs
        mixed_t.append(mm(values_t[head * size : (head + 1) * size], probs))
    mixed = jnp.concatenate(mixed_t, axis=0).T.astype(bf16)
    mixed_out[0] = mixed
    result = mm(mixed, wo[...]).astype(bf16)
    result_out[0] = result
    put_rows(mm(hot_low, (gate * result.astype(f32)).astype(bf16), TN), own, sib)


def attend_back_kernel(n, *refs):
    g_refs, refs = refs[:n], refs[n:]
    slot_ref, router_ref, mine_ref, wk, wv, wq, wo, *refs = refs
    c_ref, q_ref, k_ref, v_ref, p_ref, mixed_ref, result_ref, gate_ref, *refs = refs
    own, sib, gr_out, dq_out, dk_out, dv_out, router_out = refs
    slots, features = c_ref.shape[1:]
    size = features // HEADS
    hot = one_hot(slot_ref, slots)
    hot_low = hot.astype(f32).astype(bf16)
    gate = gate_ref[0]
    picked = mm(hot_low, rows_of(g_refs).astype(bf16))
    gr = (gate * picked).astype(bf16)
    gr_out[0] = gr
    turn = gate * jnp.sum(picked * result_ref[0].astype(f32), axis=1, keepdims=True)
    grad_mixed = mm(gr, wo[...], NT).astype(bf16)
    keys = k_ref[0]
    keys_t = keys.astype(f32).T.astype(bf16)
    queries = q_ref[0]
    values = v_ref[0]
    low = lax.broadcasted_iota(jnp.int32, (slots, 2 * size), 1) < size
    zero = jnp.zeros((slots, 2 * size), bf16)
    dq_t, dk, dv = [], [], []
    for head in range(HEADS):
        lanes = slice(head // 2 * 2 * size, (head // 2 + 1) * 2 * size)
        keep = low if head % 2 == 0 else jnp.logical_not(low)
        q_head = jnp.where(keep, queries[:, lanes], zero)
        gm_head = jnp.where(keep, grad_mixed[:, lanes], zero)
        probs = p_ref[0, head]
        dv_part = mm(probs, gm_head)
        probs_wide = probs.astype(f32)
        grad_probs = mm(values[:, lanes], gm_head, NT)
        inner = jnp.sum(probs_wide * grad_probs, axis=0, keepdims=True)
        grad_scores = (probs_wide * (grad_probs - inner)).astype(bf16)
        dq_t.append(mm(keys_t[head * size : (head + 1) * size], grad_scores))
        dk_part = mm(grad_scores, q_head)
        if head % 2 == 0:
            dk.append(dk_part)
            dv.append(dv_part)
        else:
            dk[-1] += dk_part
            dv[-1] += dv_part
    dq = (jnp.concatenate(dq_t, axis=0).T * size ** (-0.5)).astype(bf16)
    dq_out[0] = dq
    dk = jnp.concatenate(dk, axis=1).astype(bf16)
    dk_out[0] = dk
    dv = jnp.concatenate(dv, axis=1).astype(bf16)
    dv_out[0] = dv
    copies = c_ref[0].astype(f32)
    router_out[0] = jnp.sum(turn * copies, axis=0, keepdims=True)
    router_row = jnp.sum(mine_ref[...] * router_ref[0].astype(f32), axis=0, keepdims=True)
    back = mm(dq, wq[...], NT) + turn * router_row
    rows = mm(hot_low, back.astype(bf16), TN) + mm(dk, wk[...], NT) + mm(dv, wv[...], NT)
    put_rows(rows, own, sib)


def gelu_parts(hidden):
    phi = 0.5 + 0.5 * lax.erf(hidden * (0.5**0.5))
    bell = jnp.exp(-0.5 * hidden * hidden) * 0.3989422804014327
    return hidden * phi, phi + hidden * bell


def forward_body(x_refs, mask_ref, slot_ref, router_ref, mine_ref, up, down, chunk, outs):
    own, sib, c_out, active_out, slope_out, result_out, gate_out = outs
    slots = c_out.shape[1]
    x = rows_of(x_refs).astype(bf16)
    hot = one_hot(slot_ref, slots)
    hot_low = hot.astype(f32).astype(bf16)
    gate_row = own_gate(x, router_ref[0], mask_ref[0], mine_ref[...])
    gate = jnp.sum(jnp.where(hot, gate_row, 0.0), axis=1, keepdims=True)
    gate_out[0] = gate
    copies = mm(hot_low, x).astype(bf16)
    c_out[0] = copies
    total = None
    for at in range(0, up.shape[1], chunk):
        cols = slice(at, at + chunk)
        active, slope = gelu_parts(mm(copies, up[:, cols]))
        active = active.astype(bf16)
        active_out[0, :, cols] = active
        slope_out[0, :, cols] = slope.astype(bf16)
        part = mm(active, down[cols, :])
        total = part if total is None else total + part
    result = total.astype(bf16)
    result_out[0] = result
    put_rows(mm(hot_low, (gate * result.astype(f32)).astype(bf16), TN), own, sib)


def backward_body(g_refs, slot_ref, router_ref, mine_ref, up, down, chunk, kept, outs):
    c_ref, slope_ref, result_ref, gate_ref = kept
    own, sib, gr_out, gh_out, router_out = outs
    slots = c_ref.shape[1]
    hot_low = one_hot(slot_ref, slots).astype(f32).astype(bf16)
    gate = gate_ref[0]
    picked = mm(hot_low, rows_of(g_refs).astype(bf16))
    gr = (gate * picked).astype(bf16)
    gr_out[0] = gr
    turn = gate * jnp.sum(picked * result_ref[0].astype(f32), axis=1, keepdims=True)
    total = None
    for at in range(0, up.shape[1], chunk):
        cols = slice(at, at + chunk)
        gh = (mm(gr, down[cols, :], NT) * slope_ref[0, :, cols].astype(f32)).astype(bf16)
        gh_out[0, :, cols] = gh
        part = mm(gh, up[:, cols], NT)
        total = part if total is None else total + part
    router_out[0] = jnp.sum(turn * c_ref[0].astype(f32), axis=0, keepdims=True)
    router_row = jnp.sum(mine_ref[...] * router_ref[0].astype(f32), axis=0, keepdims=True)
    back = total + turn * router_row
    put_rows(mm(hot_low, back.astype(bf16), TN), own, sib)


def perceptron_kernel(n, chunk, *refs):
    x_refs, refs = refs[:n], refs[n:]
    mask_ref, slot_ref, router_ref, mine_ref, up, down, *outs = refs
    forward_body(x_refs, mask_ref, slot_ref, router_ref, mine_ref, up, down, chunk, outs)


def perceptron_back_kernel(n, chunk, *refs):
    g_refs, refs = refs[:n], refs[n:]
    slot_ref, router_ref, mine_ref, up, down, c_ref, slope, result, gate, *outs = refs
    kept = (c_ref, slope, result, gate)
    backward_body(g_refs, slot_ref, router_ref, mine_ref, up, down, chunk, kept, outs)


def perceptron_both_kernel(n, chunk, *refs):
    x_refs, g_refs, refs = refs[:n], refs[n : 2 * n], refs[2 * n :]
    mask_ref, slot_ref, router_ref, mine_ref, up, down, *refs = refs
    own, sib, c_out, active_out, own_b, sib_b, gr_out, gh_out, router_out, *refs = refs
    slope, result, gate = refs
    outs = (own, sib, c_out, active_out, slope, result, gate)
    forward_body(x_refs, mask_ref, slot_ref, router_ref, mine_ref, up, down, chunk, outs)
    kept = (c_out, slope, result, gate)
    outs = (own_b, sib_b, gr_out, gh_out, router_out)
    backward_body(g_refs, slot_ref, router_ref, mine_ref, up, down, chunk, kept, outs)


def flat(ref):
    images, rows, features = ref.shape
    return ref[...].astype(f32).reshape(images * rows, features)


def normed(state):
    centered = state - jnp.mean(state, axis=-1, keepdims=True)
    inverse = lax.rsqrt(jnp.mean(centered * centered, axis=-1, keepdims=True) + epsilon)
    return centered * inverse, inverse


def enter_kernel(state_ref, gain_ref, shift_ref, low_out):
    unit, _ = normed(flat(state_ref))
    low_out[...] = (unit * gain_ref[...] + shift_ref[...]).reshape(low_out.shape).astype(bf16)


def join_kernel(parts, last, *refs):
    part_refs, refs = refs[:parts], refs[parts:]
    state_ref, gain_ref, shift_ref, state_out, *low_out = refs
    state = flat(state_ref)
    added = flat(part_refs[0])
    for r in part_refs[1:]:
        added = added + flat(r)
    state = state + added
    state_out[...] = state.reshape(state_out.shape)
    if not last:
        unit, _ = normed(state)
        rows = unit * gain_ref[...] + shift_ref[...]
        low_out[0][...] = rows.reshape(low_out[0].shape).astype(bf16)


def join_back_kernel(parts, *refs):
    part_refs, refs = refs[:parts], refs[parts:]
    grad_ref, before_ref, after_ref, low_ref, router_ref, mask_ref, gain_ref, *refs = refs
    grad_out, low_out, gain_out, shift_out, router_out = refs
    images, rows, features = grad_ref.shape
    back = flat(part_refs[0])
    for r in part_refs[1:]:
        back = back + flat(r)
    grad = flat(grad_ref)
    before = flat(before_ref)
    share = jnp.sum(grad * (flat(after_ref) - before), axis=1, keepdims=True)
    highest = lax.Precision.HIGHEST
    taken = []
    for i in range(images):
        router = router_ref[i]
        gates = masked_softmax(mm(low_ref[i], router, NT), mask_ref[i] > 0.5, 1)
        weighted = gates * share[i * rows : (i + 1) * rows]
        taken.append(mm(weighted, router.astype(f32), NN, highest))
        router_out[i] = -mm(weighted, low_ref[i].astype(f32), TN, highest)
    back = back - jnp.concatenate(taken, axis=0)
    unit, inverse = normed(before)
    gain_out[...] = jnp.sum(back * unit, axis=0, keepdims=True)
    shift_out[...] = jnp.sum(back, axis=0, keepdims=True)
    back = back * gain_ref[...]
    back = back - jnp.mean(back, axis=1, keepdims=True)
    back = back - unit * jnp.mean(back * unit, axis=1, keepdims=True)
    grad = grad + inverse * back
    grad_out[...] = grad.reshape(grad_out.shape)
    low_out[...] = grad.reshape(low_out.shape).astype(bf16)


def pair(array, offset):
    size = lax.axis_size("expert")
    return lax.ppermute(array, "expert", [(i, i ^ offset) for i in range(size)])


def gather(array):
    size = lax.axis_size("expert")
    found = {0: array}
    for d in range(size - 2, 0, -2):
        found[d] = pair(array, d)
    for d in range(0, size, 2):
        found[d + 1] = pair(found[d], 1)
    return [found[d] for d in range(size)]


def scatter(own, sib):
    other = pair(sib, 1)
    parts = []
    for j in range(own.shape[0] - 1, -1, -1):
        both = (own[j].astype(f32) + other[j].astype(f32)).astype(bf16)
        parts.append(both if j == 0 else pair(both, 2 * j))
    return parts[::-1]


def local(
    inputs,
    attention_routes,
    perceptron_routes,
    task_index,
    attention_gain,
    attention_shift,
    perceptron_gain,
    perceptron_shift,
    key_weight,
    value_weight,
    query_weight,
    output_weight,
    up_weight,
    down_weight,
    attention_router,
    perceptron_router,
    cotangent,
):
    n = lax.axis_size("expert")
    me = lax.axis_index("expert")
    images, rows, features = inputs.shape
    layers = key_weight.shape[0]
    hidden = up_weight.shape[-1]
    top = attention_routes.shape[-1]
    tasks = attention_router.shape[1]
    capacity = min(rows, rows * top // n * 4 // 3)
    slots = n * capacity
    total = n * rows
    chunk = 384
    mine = (jnp.arange(n, dtype=jnp.int32) == me).astype(f32)[:, None]

    routes = jnp.stack([attention_routes, perceptron_routes])
    named = (routes[..., None] == jnp.arange(n, dtype=jnp.int32)).any(axis=-2)
    home_mask = named.astype(f32)
    turned = named.astype(bf16).transpose(0, 1, 2, 4, 3).reshape(-1, rows)
    all_masks = jnp.concatenate(gather(turned), axis=-1).reshape(2, layers, images, n, total)
    mine_mask = jnp.einsum(
        "kliet,e->klit", all_masks, mine[:, 0].astype(bf16), preferred_element_type=f32
    )
    blocks = mine_mask.reshape(2, layers, images, n, rows)
    earlier = jnp.tril(jnp.ones((rows, rows), bf16), -1)
    position = jnp.einsum(
        "klibr,qr->klibq", blocks.astype(bf16), earlier, preferred_element_type=f32
    )
    position = position.astype(jnp.int32) + jnp.arange(n, dtype=jnp.int32)[:, None] * capacity
    slot = jnp.where(blocks > 0.5, position, -1).reshape(2, layers, images, 1, total)
    masks = all_masks.astype(f32)
    routers = (
        attention_router[:, task_index].transpose(0, 1, 3, 2),
        perceptron_router[:, task_index].transpose(0, 1, 3, 2),
    )

    row_shape = (images, rows, features)
    part_shape = (n // 2, images, rows, features)
    slot_shape = (images, slots, features)
    all_shape = (images, total, features)
    gate_shape = (images, slots, 1)
    wide_shape = (images, slots, hidden)
    probs_shape = (images, HEADS, total, slots)
    router_shape = (images, 1, features)
    partial_rows = (part_shape, bf16, per_image_second)
    slot_rows = (slot_shape, bf16, per_image)
    all_rows = (all_shape, bf16, per_image)
    wide_rows = (wide_shape, bf16, per_image)
    gate_rows = (gate_shape, f32, per_image)
    router_rows = (router_shape, f32, per_image)
    flop_small = 2 * images * slots * features * features
    flop_core = 2 * images * slots * total * features
    flop_wide = 2 * images * slots * features * hidden

    def image(array):
        return (array, per_image)

    def const(array):
        return (array, whole)

    def join(parts, state, gain, shift):
        last = gain is None
        if last:
            gain = shift = jnp.zeros((1, features), f32)
        outs = [(row_shape, f32, whole)] + ([] if last else [(row_shape, bf16, whole)])
        ins = [const(a) for a in (*parts, state, gain, shift)]
        return run("join", partial(join_kernel, len(parts), last), 1, ins, outs, 10**6, 16)

    def join_back(parts, grad, before, after, low, router, mask, gain):
        ins = [const(a) for a in (*parts, grad, before, after, low, router, mask, gain)]
        outs = [
            (row_shape, f32, whole),
            (row_shape, bf16, whole),
            ((1, features), f32, whole),
            ((1, features), f32, whole),
            ((images, n, features), f32, whole),
        ]
        return run("join_back", partial(join_back_kernel, len(parts)), 1, ins, outs, 10**6, 16)

    state = inputs.astype(f32)
    (low,) = run(
        "enter",
        enter_kernel,
        1,
        [const(a) for a in (inputs, attention_gain[:1], attention_shift[:1])],
        [(row_shape, bf16, whole)],
        10**6,
        16,
    )
    x_all = gather(low)
    cotangent_all = gather(cotangent)
    kept = []
    for l in range(layers):
        weights = [key_weight[l], value_weight[l], query_weight[l, 0], output_weight[l, 0]]
        own, sib, *saved = run(
            "attend",
            partial(attend_kernel, n),
            images,
            [image(a) for a in x_all]
            + [image(masks[0, l]), image(slot[0, l]), image(routers[0][l]), const(mine)]
            + [const(w) for w in weights],
            [partial_rows, partial_rows, all_rows, slot_rows, slot_rows, all_rows, all_rows]
            + [(probs_shape, bf16, per_image), slot_rows, slot_rows, gate_rows],
            2 * flop_core + 6 * flop_small,
            40,
        )
        low_a = low
        middle, low = join(
            scatter(own, sib), state, perceptron_gain[l : l + 1], perceptron_shift[l : l + 1]
        )
        x_all = gather(low)
        ff_weights = [up_weight[l, 0], down_weight[l, 0]]
        route_ins = [image(masks[1, l]), image(slot[1, l]), image(routers[1][l]), const(mine)]
        last = l == layers - 1
        if not last:
            own, sib, copies, active, slope, result, gate = run(
                "perceptron",
                partial(perceptron_kernel, n, chunk),
                images,
                [image(a) for a in x_all] + route_ins + [const(w) for w in ff_weights],
                [partial_rows, partial_rows, slot_rows, wide_rows, wide_rows]
                + [slot_rows, gate_rows],
                2 * flop_wide,
                40,
            )
            kept_ff = (copies, slope, result, gate)
            after, low_next = join(
                scatter(own, sib),
                middle,
                attention_gain[l + 1 : l + 2],
                attention_shift[l + 1 : l + 2],
            )
        else:
            own, sib, copies, active, own_b, sib_b, gr, gh, router_m, _, _, _ = run(
                "perceptron_both",
                partial(perceptron_both_kernel, n, chunk),
                images,
                [image(a) for a in (*x_all, *cotangent_all)]
                + route_ins
                + [const(w) for w in ff_weights],
                [partial_rows, partial_rows, slot_rows, wide_rows, partial_rows, partial_rows]
                + [slot_rows, wide_rows, router_rows, wide_rows, slot_rows, gate_rows],
                4 * flop_wide,
                48,
            )
            kept_ff = (own_b, sib_b, gr, gh, router_m)
            (after,) = join(scatter(own, sib), middle, None, None)
            low_next = None
        kept.append((state, low_a, saved, middle, low, copies, active, kept_ff, after))
        state = after
        low = low_next
        if not last:
            x_all = gather(low)

    grad = cotangent.astype(f32)
    grad_low = None
    shared, experts = [], []
    for l in range(layers - 1, -1, -1):
        state, low_a, saved, middle, low_m, copies, active, kept_ff, after = kept[l]
        ff_weights = [up_weight[l, 0], down_weight[l, 0]]
        if l == layers - 1:
            own, sib, gr, gh, router_m = kept_ff
        else:
            own, sib, gr, gh, router_m = run(
                "perceptron_back",
                partial(perceptron_back_kernel, n, chunk),
                images,
                [image(a) for a in gather(grad_low)]
                + [image(slot[1, l]), image(routers[1][l]), const(mine)]
                + [const(w) for w in ff_weights]
                + [image(a) for a in kept_ff],
                [partial_rows, partial_rows, slot_rows, wide_rows, router_rows],
                2 * flop_wide,
                40,
            )
        down_part = jnp.einsum("isf,isd->fd", active, gr, preferred_element_type=f32)
        up_part = jnp.einsum("isd,isf->df", copies, gh, preferred_element_type=f32)
        grad, grad_low, gain_m, shift_m, router_home_m = join_back(
            scatter(own, sib),
            grad,
            middle,
            after,
            low_m,
            routers[1][l],
            home_mask[1, l],
            perceptron_gain[l : l + 1],
        )
        x, copies, queries, keys, values, probs, mixed, result, gate = saved
        weights = [key_weight[l], value_weight[l], query_weight[l, 0], output_weight[l, 0]]
        own, sib, gr, dq, dk, dv, router_a = run(
            "attend_back",
            partial(attend_back_kernel, n),
            images,
            [image(a) for a in gather(grad_low)]
            + [image(slot[0, l]), image(routers[0][l]), const(mine)]
            + [const(w) for w in weights]
            + [image(a) for a in (copies, queries, keys, values, probs, mixed, result, gate)],
            [partial_rows, partial_rows, slot_rows, slot_rows, all_rows, all_rows, router_rows],
            4 * flop_core + 10 * flop_small,
            48,
        )
        output_part = jnp.einsum("isf,isd->fd", mixed, gr, preferred_element_type=f32)
        query_part = jnp.einsum("isd,isf->df", copies, dq, preferred_element_type=f32)
        key_part = jnp.einsum("itd,itf->df", x, dk, preferred_element_type=f32)
        value_part = jnp.einsum("itd,itf->df", x, dv, preferred_element_type=f32)
        grad, grad_low, gain_a, shift_a, router_home_a = join_back(
            scatter(own, sib),
            grad,
            state,
            middle,
            low_a,
            routers[0][l],
            home_mask[0, l],
            attention_gain[l : l + 1],
        )
        router_a = router_home_a + mine * router_a
        router_m = router_home_m + mine * router_m
        shared.append((gain_a, shift_a, gain_m, shift_m, key_part, value_part, router_a, router_m))
        experts.append((query_part, output_part, up_part, down_part))

    picked = (task_index[:, None] == jnp.arange(tasks, dtype=jnp.int32)[None, :]).astype(f32)
    experts = [
        jnp.stack([lax.psum(v.astype(bf16), "dp").astype(f32) for v in items[::-1]])[:, None]
        for items in zip(*experts)
    ]
    shared = [jnp.stack(items[::-1]) for items in zip(*shared)]
    gains = [a[:, 0] for a in shared[:4]]
    routers = [
        jnp.einsum("it,lied->ltde", picked, a, precision=lax.Precision.HIGHEST)
        for a in shared[6:]
    ]
    shared = lax.psum((*gains, shared[4], shared[5], *routers), ("dp", "expert"))
    return (after_last(kept), grad, *shared[:6], *experts, *shared[6:])


def after_last(kept):
    return kept[-1][-1]


def solution(mesh):
    in_specs = (
        P("dp", "expert", None),
        P(None, "dp", "expert", None),
        P(None, "dp", "expert", None),
        P("dp"),
        P(),
        P(),
        P(),
        P(),
        P(),
        P(),
        P(None, "expert", None, None),
        P(None, "expert", None, None),
        P(None, "expert", None, None),
        P(None, "expert", None, None),
        P(),
        P(),
        P("dp", "expert", None),
    )
    out_specs = (
        P("dp", "expert", None),
        P("dp", "expert", None),
        P(),
        P(),
        P(),
        P(),
        P(),
        P(),
        P(None, "expert", None, None),
        P(None, "expert", None, None),
        P(None, "expert", None, None),
        P(None, "expert", None, None),
        P(),
        P(),
    )
    return jax.shard_map(local, mesh=mesh, in_specs=in_specs, out_specs=out_specs, check_vma=False)
```

```python
from functools import partial

import jax
import jax.numpy as jnp
from jax import lax
from jax.experimental import pallas as pl
from jax.experimental.pallas import tpu as pltpu
from jax.sharding import PartitionSpec as P

HEADS = 6
epsilon = 1e-06
f32, bf16 = jnp.float32, jnp.bfloat16
NN, NT, TN = ((1,), (0,)), ((1,), (1,)), ((0,), (0,))
MIB = 1 << 20


def mm(left, right, dims=NN, precision=None):
    return lax.dot_general(
        left, right, (dims, ((), ())), preferred_element_type=f32, precision=precision
    )


def whole(array):
    rank = len(array.shape)
    return pl.BlockSpec(array.shape, lambda i: (0,) * rank)


def per_image(array):
    rank = len(array.shape)
    return pl.BlockSpec((1,) + tuple(array.shape[1:]), lambda i: (i,) + (0,) * (rank - 1))


def per_image_second(array):
    rank = len(array.shape)
    return pl.BlockSpec(
        (array.shape[0], 1) + tuple(array.shape[2:]), lambda i: (0, i) + (0,) * (rank - 2)
    )


def at_layer(layer):
    def maker(array):
        rank = len(array.shape)
        lead = rank - 2
        return pl.BlockSpec(
            (None,) * lead + tuple(array.shape[lead:]),
            lambda i: (layer,) + (0,) * (rank - 1),
        )

    return maker


def in_smem(array):
    return pl.BlockSpec(memory_space=pltpu.SMEM)


def run(name, kernel, images, ins, outs, flops, limit, scratch=()):
    shapes = [jax.ShapeDtypeStruct(shape, dtype) for shape, dtype, *_ in outs]
    moved = sum(a.size * a.dtype.itemsize for a, _ in ins)
    moved += sum(s.size * s.dtype.itemsize for s in shapes)
    out_specs = [item[2](s) for s, item in zip(shapes, outs)]
    shapes = [pltpu.HBM(*item[:2]) if len(item) > 3 else s for s, item in zip(shapes, outs)]
    return pl.pallas_call(
        kernel,
        grid=(images,),
        in_specs=[maker(a) for a, maker in ins],
        out_specs=out_specs,
        out_shape=shapes,
        scratch_shapes=list(scratch),
        compiler_params=pltpu.CompilerParams(
            dimension_semantics=("arbitrary",), vmem_limit_bytes=limit * MIB
        ),
        cost_estimate=pl.CostEstimate(flops=1, bytes_accessed=1, transcendentals=0),
        name=name,
    )(*[a for a, _ in ins])


def rows_of(refs, rows=None):
    return jnp.concatenate([r[0].astype(f32)[:rows] for r in refs], axis=0)


def home_of(refs, rows, mine):
    total = refs[0][0].astype(f32)[rows:]
    for r in refs[1:]:
        total = total + r[0].astype(f32)[rows:]
    return jnp.sum(total * mine, axis=0, keepdims=True)


def put_rows(rows, own_ref, sib_ref):
    half = own_ref.shape[0]
    size = own_ref.shape[2]
    for d in range(2 * half):
        target = own_ref if d % 2 == 0 else sib_ref
        target[d // 2, 0] = rows[d * size : (d + 1) * size].astype(bf16)


def one_hot(slot_ref, slots):
    slot = slot_ref[0]
    spots = lax.broadcasted_iota(jnp.int32, (slots, slot.shape[1]), 0)
    return spots == slot


def masked_softmax(logits, mask, axis):
    top = jnp.max(jnp.where(mask, logits, -3e38), axis=axis, keepdims=True)
    weights = jnp.where(mask, jnp.exp(jnp.minimum(logits - top, 0.0)), 0.0)
    return weights / jnp.sum(weights, axis=axis, keepdims=True)


def own_gate(rows_low, router, mask8, mine):
    gates = masked_softmax(mm(router, rows_low, NT), mask8 > 0.5, 0)
    return jnp.sum(gates * mine, axis=0, keepdims=True)


def attend_kernel(n, *refs):
    x_refs, refs = refs[:n], refs[n:]
    mask_ref, slot_ref, router_ref, mine_ref, wk, wv, wq, wo, *refs = refs
    own, sib, x_out, c_out, q_out, k_out, v_out, p_out, mixed_out, result_out, gate_out = refs
    slots, features = c_out.shape[1:]
    size = features // HEADS
    x = rows_of(x_refs).astype(bf16)
    x_out[0] = x
    hot = one_hot(slot_ref, slots)
    hot_low = hot.astype(f32).astype(bf16)
    gate_row = own_gate(x, router_ref[0], mask_ref[0], mine_ref[...])
    gate = jnp.sum(jnp.where(hot, gate_row, 0.0), axis=1, keepdims=True)
    gate_out[0] = gate
    copies = mm(hot_low, x).astype(bf16)
    c_out[0] = copies
    queries = (mm(copies, wq[...]).astype(bf16).astype(f32) * size ** (-0.5)).astype(bf16)
    q_out[0] = queries
    keys = mm(x, wk[...]).astype(bf16)
    k_out[0] = keys
    values = mm(x, wv[...])
    v_out[0] = values.astype(bf16)
    values_t = values.T.astype(bf16)
    low = lax.broadcasted_iota(jnp.int32, (slots, 2 * size), 1) < size
    zero = jnp.zeros((slots, 2 * size), bf16)
    mixed_t = []
    for head in range(HEADS):
        lanes = slice(head // 2 * 2 * size, (head // 2 + 1) * 2 * size)
        q_head = jnp.where(low if head % 2 == 0 else jnp.logical_not(low), queries[:, lanes], zero)
        scores = mm(keys[:, lanes], q_head, NT)
        weights = jnp.exp(scores - jnp.max(scores, axis=0, keepdims=True))
        inverse = 1.0 / jnp.sum(weights, axis=0, keepdims=True)
        probs = (weights * inverse).astype(bf16)
        p_out[0, head] = probs
        mixed_t.append(mm(values_t[head * size : (head + 1) * size], probs))
    mixed = jnp.concatenate(mixed_t, axis=0).T.astype(bf16)
    mixed_out[0] = mixed
    result = mm(mixed, wo[...]).astype(bf16)
    result_out[0] = result
    put_rows(mm(hot_low, (gate * result.astype(f32)).astype(bf16), TN), own, sib)


def attend_back_kernel(n, rows, *refs):
    g_refs, refs = refs[:n], refs[n:]
    me_ref, slot_ref, router_ref, mine_ref, wk, wv, wq, wo, *refs = refs
    x_ref, c_ref, q_ref, k_ref, v_ref, p_ref, mixed_ref, result_ref, gate_ref, *refs = refs
    own, sib, gr_out, dq_out, router_out, home_out, key_sum, value_sum = refs
    image = pl.program_id(0)
    slots, features = c_ref.shape[1:]
    size = features // HEADS
    hot = one_hot(slot_ref, slots)
    hot_low = hot.astype(f32).astype(bf16)
    gate = gate_ref[0]
    picked = mm(hot_low, rows_of(g_refs, rows).astype(bf16))
    home_out[0] = home_of(g_refs, rows, mine_ref[...])
    gr = (gate * picked).astype(bf16)
    gr_out[0] = gr
    turn = gate * jnp.sum(picked * result_ref[0].astype(f32), axis=1, keepdims=True)
    grad_mixed = mm(gr, wo[...], NT).astype(bf16)
    keys = k_ref[0]
    keys_t = keys.astype(f32).T.astype(bf16)
    queries = q_ref[0]
    values = v_ref[0]
    low = lax.broadcasted_iota(jnp.int32, (slots, 2 * size), 1) < size
    zero = jnp.zeros((slots, 2 * size), bf16)
    dq_t, dk, dv = [], [], []
    for head in range(HEADS):
        lanes = slice(head // 2 * 2 * size, (head // 2 + 1) * 2 * size)
        keep = low if head % 2 == 0 else jnp.logical_not(low)
        q_head = jnp.where(keep, queries[:, lanes], zero)
        gm_head = jnp.where(keep, grad_mixed[:, lanes], zero)
        probs = p_ref[0, head]
        dv_part = mm(probs, gm_head)
        probs_wide = probs.astype(f32)
        grad_probs = mm(values[:, lanes], gm_head, NT)
        inner = jnp.sum(probs_wide * grad_probs, axis=0, keepdims=True)
        grad_scores = (probs_wide * (grad_probs - inner)).astype(bf16)
        dq_t.append(mm(keys_t[head * size : (head + 1) * size], grad_scores))
        dk_part = mm(grad_scores, q_head)
        if head % 2 == 0:
            dk.append(dk_part)
            dv.append(dv_part)
        else:
            dk[-1] += dk_part
            dv[-1] += dv_part
    dq = (jnp.concatenate(dq_t, axis=0).T * size ** (-0.5)).astype(bf16)
    dq_out[0] = dq
    dk = jnp.concatenate(dk, axis=1).astype(bf16)
    dv = jnp.concatenate(dv, axis=1).astype(bf16)
    copies = c_ref[0].astype(f32)
    router_out[0] = jnp.sum(turn * copies, axis=0, keepdims=True)
    router_row = jnp.sum(mine_ref[...] * router_ref[0].astype(f32), axis=0, keepdims=True)
    back = mm(dq, wq[...], NT) + turn * router_row
    back = mm(hot_low, back.astype(bf16), TN) + mm(dk, wk[...], NT) + mm(dv, wv[...], NT)
    step = -(-rows // 16) * 16
    at = pl.ds(pl.multiple_of(image * step, 16), step)
    gap = jnp.zeros((step - rows, features), f32)
    for d in range(n):
        target = own if d % 2 == 0 else sib
        part = back[d * rows : (d + 1) * rows]
        if step > rows:
            part = jnp.concatenate([part, gap], axis=0)
        target[d // 2, at, :] = part.astype(bf16)
    key_part, value_part = mm(x_ref[0], dk, TN), mm(x_ref[0], dv, TN)

    @pl.when(image == 0)
    def _():
        key_sum[...] = key_part
        value_sum[...] = value_part

    @pl.when(image > 0)
    def _():
        key_sum[...] += key_part
        value_sum[...] += value_part

    @pl.when(image == pl.num_programs(0) - 1)
    def _():
        share = features // n
        start = own.shape[1] - 2 * share
        for d in range(n):
            target = own if d % 2 == 0 else sib
            taken = pl.ds(pl.multiple_of((me_ref[0] ^ d) * share, 8), share)
            both = jnp.concatenate([key_sum[taken, :], value_sum[taken, :]], axis=0)
            target[d // 2, start:, :] = both.astype(bf16)


def gelu_parts(hidden):
    phi = 0.5 + 0.5 * lax.erf(hidden * (0.5**0.5))
    bell = jnp.exp(-0.5 * hidden * hidden) * 0.3989422804014327
    return hidden * phi, phi + hidden * bell


def forward_body(x_refs, mask_ref, slot_ref, router_ref, mine_ref, up, down, chunk, outs):
    own, sib, c_out, active_out, slope_out, result_out, gate_out = outs
    slots = c_out.shape[1]
    x = rows_of(x_refs).astype(bf16)
    hot = one_hot(slot_ref, slots)
    hot_low = hot.astype(f32).astype(bf16)
    gate_row = own_gate(x, router_ref[0], mask_ref[0], mine_ref[...])
    gate = jnp.sum(jnp.where(hot, gate_row, 0.0), axis=1, keepdims=True)
    gate_out[0] = gate
    copies = mm(hot_low, x).astype(bf16)
    c_out[0] = copies
    total = None
    for at in range(0, up.shape[1], chunk):
        cols = slice(at, at + chunk)
        active, slope = gelu_parts(mm(copies, up[:, cols]))
        active = active.astype(bf16)
        active_out[0, :, cols] = active
        slope_out[0, :, cols] = slope.astype(bf16)
        part = mm(active, down[cols, :])
        total = part if total is None else total + part
    result = total.astype(bf16)
    result_out[0] = result
    put_rows(mm(hot_low, (gate * result.astype(f32)).astype(bf16), TN), own, sib)


def backward_body(g_refs, rows, slot_ref, router_ref, mine_ref, up, down, chunk, kept, outs):
    c_ref, slope_ref, result_ref, gate_ref = kept
    own, sib, gr_out, gh_out, router_out = outs
    slots = c_ref.shape[1]
    hot_low = one_hot(slot_ref, slots).astype(f32).astype(bf16)
    gate = gate_ref[0]
    picked = mm(hot_low, rows_of(g_refs, rows).astype(bf16))
    gr = (gate * picked).astype(bf16)
    gr_out[0] = gr
    turn = gate * jnp.sum(picked * result_ref[0].astype(f32), axis=1, keepdims=True)
    total = None
    for at in range(0, up.shape[1], chunk):
        cols = slice(at, at + chunk)
        gh = (mm(gr, down[cols, :], NT) * slope_ref[0, :, cols].astype(f32)).astype(bf16)
        gh_out[0, :, cols] = gh
        part = mm(gh, up[:, cols], NT)
        total = part if total is None else total + part
    router_out[0] = jnp.sum(turn * c_ref[0].astype(f32), axis=0, keepdims=True)
    router_row = jnp.sum(mine_ref[...] * router_ref[0].astype(f32), axis=0, keepdims=True)
    back = total + turn * router_row
    put_rows(mm(hot_low, back.astype(bf16), TN), own, sib)


def perceptron_kernel(n, chunk, *refs):
    x_refs, refs = refs[:n], refs[n:]
    mask_ref, slot_ref, router_ref, mine_ref, up, down, *outs = refs
    forward_body(x_refs, mask_ref, slot_ref, router_ref, mine_ref, up, down, chunk, outs)


def perceptron_back_kernel(n, rows, chunk, *refs):
    g_refs, refs = refs[:n], refs[n:]
    slot_ref, router_ref, mine_ref, up, down, c_ref, slope, result, gate, *outs = refs
    *outs, home_out = outs
    home_out[0] = home_of(g_refs, rows, mine_ref[...])
    kept = (c_ref, slope, result, gate)
    backward_body(g_refs, rows, slot_ref, router_ref, mine_ref, up, down, chunk, kept, outs)


def perceptron_both_kernel(n, chunk, *refs):
    x_refs, g_refs, refs = refs[:n], refs[n : 2 * n], refs[2 * n :]
    mask_ref, slot_ref, router_ref, mine_ref, up, down, *refs = refs
    own, sib, c_out, active_out, own_b, sib_b, gr_out, gh_out, router_out, *refs = refs
    slope, result, gate = refs
    outs = (own, sib, c_out, active_out, slope, result, gate)
    forward_body(x_refs, mask_ref, slot_ref, router_ref, mine_ref, up, down, chunk, outs)
    kept = (c_out, slope, result, gate)
    outs = (own_b, sib_b, gr_out, gh_out, router_out)
    backward_body(g_refs, None, slot_ref, router_ref, mine_ref, up, down, chunk, kept, outs)


def ff_gradient_kernel(given, c_ref, gr_ref, up, down, *refs):
    up_out, down_out = refs[given:]
    images, slots, features = c_ref.shape
    copies = c_ref[...].reshape(images * slots, features)
    gr = gr_ref[...].reshape(images * slots, features)
    active, slope = gelu_parts(mm(up[...], copies, ((0,), (1,))))
    gh = (mm(down[...], gr, NT) * slope).astype(bf16)
    up_out[...] = mm(gh, copies).T
    down_out[...] = mm(active.astype(bf16), gr)


def ff_gradient(copies, gr, up, down, layer, width, start, steps, before):
    features = up.shape[2]
    given = len(before)
    shapes = [jax.ShapeDtypeStruct(a.shape, f32) for a in (up, down)]
    specs = [
        pl.BlockSpec((None, None, features, width), lambda j: (layer, 0, 0, start + j)),
        pl.BlockSpec((None, None, width, features), lambda j: (layer, 0, start + j, 0)),
    ]
    return pl.pallas_call(
        partial(ff_gradient_kernel, given),
        grid=(steps,),
        in_specs=[whole(copies), whole(gr)]
        + specs
        + [pl.BlockSpec(memory_space=pl.ANY)] * given,
        out_specs=specs,
        out_shape=shapes,
        input_output_aliases={4 + j: j for j in range(given)},
        compiler_params=pltpu.CompilerParams(
            dimension_semantics=("arbitrary",), vmem_limit_bytes=60 * MIB
        ),
        cost_estimate=pl.CostEstimate(
            flops=12 * gr.size * width * steps, bytes_accessed=4 * gr.size, transcendentals=0
        ),
        name="ff_gradient",
    )(copies, gr, up, down, *before)


def assemble_kernel(n, layers, tasks, me_ref, *refs):
    found, (key_out, value_out, column_out, vector_out, late_out) = refs[:n], refs[n:]
    share = key_out.shape[1] // n
    columns, vectors, late = column_out.shape[1], vector_out.shape[0], late_out.shape[0]
    at = layers * 2 * share
    vector_sum = late_sum = 0.0
    for d in range(n):
        place = me_ref[0] ^ d
        held = found[d][...].astype(f32)
        rows = pl.ds(pl.multiple_of(place * share, 8), share)
        for layer in range(layers):
            key_out[layer, rows, :] = held[2 * layer * share : (2 * layer + 1) * share]
            value_out[layer, rows, :] = held[(2 * layer + 1) * share : (2 * layer + 2) * share]
        late_sum = late_sum + held[at : at + late]
        vector_sum = vector_sum + held[at + late : at + late + vectors]
        column_out[place] = held[at + late + vectors : at + late + vectors + columns]
    vector_out[...] = vector_sum
    late_out[...] = late_sum


def flat(ref):
    images, rows, features = ref.shape
    return ref[...].astype(f32).reshape(images * rows, features)


def normed(state):
    centered = state - jnp.mean(state, axis=-1, keepdims=True)
    inverse = lax.rsqrt(jnp.mean(centered * centered, axis=-1, keepdims=True) + epsilon)
    return centered * inverse, inverse


def enter_kernel(state_ref, gain_ref, shift_ref, low_out):
    unit, _ = normed(flat(state_ref))
    low_out[...] = (unit * gain_ref[...] + shift_ref[...]).reshape(low_out.shape).astype(bf16)


def join_kernel(parts, last, *refs):
    part_refs, refs = refs[:parts], refs[parts:]
    state_ref, gain_ref, shift_ref, state_out, *low_out = refs
    state = flat(state_ref)
    added = flat(part_refs[0])
    for r in part_refs[1:]:
        added = added + flat(r)
    state = state + added
    state_out[...] = state.reshape(state_out.shape)
    if not last:
        unit, _ = normed(state)
        rows = unit * gain_ref[...] + shift_ref[...]
        low_out[0][...] = rows.reshape(low_out[0].shape).astype(bf16)


def join_back_kernel(parts, *refs):
    part_refs, refs = refs[:parts], refs[parts:]
    grad_ref, before_ref, after_ref, low_ref, router_ref, mask_ref, gain_ref, *refs = refs
    grad_out, low_out, gain_out, shift_out, *more = refs
    images, rows, features = grad_ref.shape
    total = part_refs[0][...].astype(f32)
    for r in part_refs[1:]:
        total = total + r[...].astype(f32)
    if total.ndim == 3:
        (home_out,) = more
        back = total.reshape(images * rows, features)
    else:
        home_out, share_out = more
        step = -(-rows // 16) * 16
        back = jnp.concatenate([total[i * step : i * step + rows] for i in range(images)], axis=0)
        share_out[...] = total[images * step :].astype(bf16)
    grad = flat(grad_ref)
    before = flat(before_ref)
    share = jnp.sum(grad * (flat(after_ref) - before), axis=1, keepdims=True)
    highest = lax.Precision.HIGHEST
    taken, homes = [], []
    for i in range(images):
        router = router_ref[i]
        gates = masked_softmax(mm(low_ref[i], router, NT), mask_ref[i] > 0.5, 1)
        weighted = gates * share[i * rows : (i + 1) * rows]
        taken.append(mm(weighted, router.astype(f32), NN, highest))
        homes.append(-mm(weighted, low_ref[i].astype(f32), TN, highest))
        home_out[i] = homes[-1]
    back = back - jnp.concatenate(taken, axis=0)
    unit, inverse = normed(before)
    gain_out[...] = jnp.sum(back * unit, axis=0, keepdims=True)
    shift_out[...] = jnp.sum(back, axis=0, keepdims=True)
    back = back * gain_ref[...]
    back = back - jnp.mean(back, axis=1, keepdims=True)
    back = back - unit * jnp.mean(back * unit, axis=1, keepdims=True)
    grad = grad + inverse * back
    grad_out[...] = grad.reshape(grad_out.shape)
    for i in range(images):
        sent = jnp.concatenate([grad[i * rows : (i + 1) * rows], homes[i]], axis=0)
        low_out[i] = sent.astype(bf16)


def pair(array, offset):
    size = lax.axis_size("expert")
    return lax.ppermute(array, "expert", [(i, i ^ offset) for i in range(size)])


def gather(array):
    size = lax.axis_size("expert")
    found = {0: array}
    for d in range(size - 2, 0, -2):
        found[d] = pair(array, d)
    for d in range(0, size, 2):
        found[d + 1] = pair(found[d], 1)
    return [found[d] for d in range(size)]


def scatter(own, sib):
    other = pair(sib, 1)
    parts = []
    for j in range(own.shape[0] - 1, -1, -1):
        both = (own[j].astype(f32) + other[j].astype(f32)).astype(bf16)
        parts.append(both if j == 0 else pair(both, 2 * j))
    return parts[::-1]


def add_low(left, right):
    return (left.astype(f32) + right.astype(f32)).astype(bf16)


def dp_pair(array, offset):
    size = lax.axis_size("dp")
    return lax.ppermute(array, "dp", [(i, i ^ offset) for i in range(size)])


def dp_add(array, beside):
    size = lax.axis_size("dp")
    if size & (size - 1):
        return lax.psum(array, "dp")
    offset = 1
    while offset < size:
        arrived = [dp_pair(array, offset)]
        offset *= 2
        if offset >= size:
            beside(arrived)
        array = add_low(array, arrived[0])
    return array


def local(
    inputs,
    attention_routes,
    perceptron_routes,
    task_index,
    attention_gain,
    attention_shift,
    perceptron_gain,
    perceptron_shift,
    key_weight,
    value_weight,
    query_weight,
    output_weight,
    up_weight,
    down_weight,
    attention_router,
    perceptron_router,
    cotangent,
):
    n = lax.axis_size("expert")
    me = lax.axis_index("expert").astype(jnp.int32)
    me_dp = lax.axis_index("dp").astype(jnp.int32)[None]
    dp = lax.axis_size("dp")
    images, rows, features = inputs.shape
    layers = key_weight.shape[0]
    hidden = up_weight.shape[-1]
    few = dp & (dp - 1) == 0 and dp <= 4 and features % (16 * dp) == 0
    copies_all, gr_all = {}, {}
    top = attention_routes.shape[-1]
    tasks = attention_router.shape[1]
    capacity = min(rows, rows * top // n * 4 // 3)
    slots = n * capacity
    total = n * rows
    chunk = 384
    width, steps = 256, 6
    mine = (jnp.arange(n, dtype=jnp.int32) == me).astype(f32)[:, None]

    routes = jnp.stack([attention_routes, perceptron_routes])
    named = (routes[..., None] == jnp.arange(n, dtype=jnp.int32)).any(axis=-2)
    home_mask = named.astype(f32)
    turned = named.astype(bf16).transpose(0, 1, 2, 4, 3).reshape(-1, rows)
    all_masks = jnp.concatenate(gather(turned), axis=-1).reshape(2, layers, images, n, total)
    mine_mask = jnp.einsum(
        "kliet,e->klit", all_masks, mine[:, 0].astype(bf16), preferred_element_type=f32
    )
    blocks = mine_mask.reshape(2, layers, images, n, rows)
    earlier = jnp.tril(jnp.ones((rows, rows), bf16), -1)
    position = jnp.einsum(
        "klibr,qr->klibq", blocks.astype(bf16), earlier, preferred_element_type=f32
    )
    position = position.astype(jnp.int32) + jnp.arange(n, dtype=jnp.int32)[:, None] * capacity
    slot = jnp.where(blocks > 0.5, position, -1).reshape(2, layers, images, 1, total)
    masks = all_masks.astype(f32)
    routers = (
        attention_router[:, task_index].transpose(0, 1, 3, 2),
        perceptron_router[:, task_index].transpose(0, 1, 3, 2),
    )

    row_shape = (images, rows, features)
    part_shape = (n // 2, images, rows, features)
    slot_shape = (images, slots, features)
    all_shape = (images, total, features)
    gate_shape = (images, slots, 1)
    wide_shape = (images, slots, hidden)
    probs_shape = (images, HEADS, total, slots)
    router_shape = (images, 1, features)
    part_rows = features // n
    step = -(-rows // 16) * 16
    back_shape = (n // 2, images * step + 2 * part_rows, features)
    partial_rows = (part_shape, bf16, per_image_second)
    slot_rows = (slot_shape, bf16, per_image, "hbm")
    all_rows = (all_shape, bf16, per_image, "hbm")
    wide_rows = (wide_shape, bf16, per_image, "hbm")
    gate_rows = (gate_shape, f32, per_image, "hbm")
    router_rows = (router_shape, f32, per_image)
    flop_small = 2 * images * slots * features * features
    flop_core = 2 * images * slots * total * features
    flop_wide = 2 * images * slots * features * hidden

    def image(array):
        return (array, per_image)

    def const(array):
        return (array, whole)

    def join(parts, state, gain, shift):
        last = gain is None
        if last:
            gain = shift = jnp.zeros((1, features), f32)
        outs = [(row_shape, f32, whole)] + ([] if last else [(row_shape, bf16, whole)])
        ins = [const(a) for a in (*parts, state, gain, shift)]
        return run("join", partial(join_kernel, len(parts), last), 1, ins, outs, 10**6, 16)

    def join_back(parts, grad, before, after, low, router, mask, gain):
        ins = [const(a) for a in (*parts, grad, before, after, low, router, mask, gain)]
        outs = [
            (row_shape, f32, whole),
            ((images, rows + n, features), bf16, whole),
            ((1, features), f32, whole),
            ((1, features), f32, whole),
            ((images, n, features), f32, whole),
        ]
        if parts[0].ndim == 2:
            outs.append(((2 * part_rows, features), bf16, whole))
        return run("join_back", partial(join_back_kernel, len(parts)), 1, ins, outs, 10**6, 16)

    state = inputs.astype(f32)
    (low,) = run(
        "enter",
        enter_kernel,
        1,
        [const(a) for a in (inputs, attention_gain[:1], attention_shift[:1])],
        [(row_shape, bf16, whole)],
        10**6,
        16,
    )
    x_all = gather(low)
    cotangent_all = gather(cotangent)
    kept = []
    for l in range(layers):
        weights = [key_weight, value_weight, query_weight, output_weight]
        own, sib, *saved = run(
            "attend",
            partial(attend_kernel, n),
            images,
            [image(a) for a in x_all]
            + [image(masks[0, l]), image(slot[0, l]), image(routers[0][l]), const(mine)]
            + [(w, at_layer(l)) for w in weights],
            [partial_rows, partial_rows, all_rows, slot_rows, slot_rows, all_rows, all_rows]
            + [(probs_shape, bf16, per_image, "hbm"), slot_rows, slot_rows, gate_rows],
            2 * flop_core + 6 * flop_small,
            60,
        )
        low_a = low
        middle, low = join(
            scatter(own, sib), state, perceptron_gain[l : l + 1], perceptron_shift[l : l + 1]
        )
        x_all = gather(low)
        ff_weights = [up_weight, down_weight]
        route_ins = [image(masks[1, l]), image(slot[1, l]), image(routers[1][l]), const(mine)]
        last = l == layers - 1
        if not last:
            own, sib, copies, active, slope, result, gate = run(
                "perceptron",
                partial(perceptron_kernel, n, chunk),
                images,
                [image(a) for a in x_all] + route_ins + [(w, at_layer(l)) for w in ff_weights],
                [partial_rows, partial_rows, slot_rows, wide_rows, wide_rows]
                + [slot_rows, gate_rows],
                2 * flop_wide,
                60,
            )
            kept_ff = (copies, slope, result, gate)
            if few:
                copies_all[l] = lax.all_gather(copies, "dp", axis=0, tiled=True)
            after, low_next = join(
                scatter(own, sib),
                middle,
                attention_gain[l + 1 : l + 2],
                attention_shift[l + 1 : l + 2],
            )
        else:
            for j in copies_all:
                x_all[-1], copies_all[j] = lax.optimization_barrier((x_all[-1], copies_all[j]))
            own, sib, copies, active, own_b, sib_b, gr, gh, router_m, _, _, _ = run(
                "perceptron_both",
                partial(perceptron_both_kernel, n, chunk),
                images,
                [image(a) for a in (*x_all, *cotangent_all)]
                + route_ins
                + [(w, at_layer(l)) for w in ff_weights],
                [partial_rows, partial_rows, slot_rows, wide_rows, partial_rows, partial_rows]
                + [slot_rows, wide_rows, router_rows, wide_rows, slot_rows, gate_rows],
                4 * flop_wide,
                60,
            )
            kept_ff = (own_b, sib_b, gr, gh, router_m)
            (after,) = join(scatter(own, sib), middle, None, None)
            low_next = None
        kept.append((state, low_a, saved, middle, low, copies, active, kept_ff, after))
        state = after
        low = low_next
        if not last:
            x_all = gather(low)

    grad = cotangent.astype(f32)
    grad_low = None
    gains, columns, shares, ff_parts, qo_parts = [], [], [], [], []
    for l in range(layers - 1, -1, -1):
        state, low_a, saved, middle, low_m, copies, active, kept_ff, after = kept[l]
        ff_weights = [up_weight, down_weight]
        if l == layers - 1:
            own, sib, gr, gh, router_m = kept_ff
        else:
            own, sib, gr, gh, router_m, home = run(
                "perceptron_back",
                partial(perceptron_back_kernel, n, rows, chunk),
                images,
                [image(a) for a in gather(grad_low)]
                + [image(slot[1, l]), image(routers[1][l]), const(mine)]
                + [(w, at_layer(l)) for w in ff_weights]
                + [image(a) for a in kept_ff],
                [partial_rows, partial_rows, slot_rows, wide_rows, router_rows, router_rows],
                2 * flop_wide,
                60,
            )
            columns[-1] = columns[-1] + home
        parts = scatter(own, sib)
        if few:
            if l == layers - 1:
                copies_all[l] = lax.all_gather(copies, "dp", axis=0, tiled=True)
            else:
                parts[-1], gr_all[l + 1] = lax.optimization_barrier((parts[-1], gr_all[l + 1]))
            gr_all[l] = lax.all_gather(gr, "dp", axis=0, tiled=True)
        else:
            up_part = jnp.einsum("isd,isf->df", copies, gh, preferred_element_type=f32)
            down_part = jnp.einsum("isf,isd->fd", active, gr, preferred_element_type=f32)
            both = (up_part.astype(bf16), down_part.astype(bf16))
            ff_parts.append(lax.psum(both, "dp"))
        grad, grad_low, gain_m, shift_m, _ = join_back(
            parts,
            grad,
            middle,
            after,
            low_m,
            routers[1][l],
            home_mask[1, l],
            perceptron_gain[l : l + 1],
        )
        columns.append(router_m)
        g_all = gather(grad_low)
        x, copies, queries, keys, values, probs, mixed, result, gate = saved
        weights = [key_weight, value_weight, query_weight, output_weight]
        own, sib, gr_a, dq, router_a, home = run(
            "attend_back",
            partial(attend_back_kernel, n, rows),
            images,
            [image(a) for a in g_all]
            + [(me[None], in_smem)]
            + [image(slot[0, l]), image(routers[0][l]), const(mine)]
            + [(w, at_layer(l)) for w in weights]
            + [image(a) for a in (x, copies, queries, keys, values, probs, mixed, result, gate)],
            [(back_shape, bf16, whole), (back_shape, bf16, whole)]
            + [slot_rows, slot_rows, router_rows, router_rows],
            4 * flop_core + 14 * flop_small,
            60,
            [pltpu.VMEM((features, features), f32)] * 2,
        )
        columns[-1] = columns[-1] + home
        columns.append(router_a)
        if few:
            held = copies_all if l == layers - 1 else gr_all
            if l == layers - 1:
                own, sib, held[l] = lax.optimization_barrier((own, sib, held[l]))
        parts = scatter(own, sib)
        both = (
            jnp.einsum("isd,isf->df", copies, dq, preferred_element_type=f32).astype(bf16),
            jnp.einsum("isf,isd->fd", mixed, gr_a, preferred_element_type=f32).astype(bf16),
        )
        parts[-1], *both = lax.optimization_barrier((parts[-1], *both))
        qo_parts.append(both)
        if few and l < layers - 1:
            parts[-1], gr_all[l] = lax.optimization_barrier((parts[-1], gr_all[l]))
        grad, grad_low, gain_a, shift_a, late, share = join_back(
            parts,
            grad,
            state,
            middle,
            low_a,
            routers[0][l],
            home_mask[0, l],
            attention_gain[l : l + 1],
        )
        gains.append((gain_a, shift_a, gain_m, shift_m))
        shares.append(share)

    if few:
        qo_parts, gr_all[0] = lax.optimization_barrier((qo_parts, gr_all[0]))

    experts = [
        jnp.stack(items[::-1]).astype(f32)[:, None] for items in zip(*lax.psum(qo_parts, "dp"))
    ]
    written = [()]
    waiting = list(range(layers)) if few else []

    def ff_step(arrived):
        if waiting:
            l = waiting.pop()
            written[0] = ff_gradient(
                copies_all[l], gr_all[l], up_weight, down_weight, l, width, 0, steps, written[0]
            )
            arrived[-1], written[0] = lax.optimization_barrier((arrived[-1], written[0]))

    picked = (task_index[:, None] == jnp.arange(tasks, dtype=jnp.int32)[None, :]).astype(f32)
    highest = lax.Precision.HIGHEST
    columns = jnp.stack([c[:, 0] for c in columns[::-1]])
    columns = jnp.einsum("it,lid->ltd", picked, columns, precision=highest)
    late = jnp.einsum("it,ied->ted", picked, late, precision=highest)
    vectors = [v for items in gains[::-1] for v in items]
    payload = [
        *shares[::-1],
        late.reshape(tasks * n, features).astype(bf16),
        *[v.astype(bf16) for v in vectors],
        columns.reshape(layers * 2 * tasks, features).astype(bf16),
    ]
    used = sum(p.shape[0] for p in payload)
    payload.append(jnp.zeros((-used % 16, features), bf16))
    shared = dp_add(jnp.concatenate(payload, axis=0), ff_step)
    found = gather(shared)
    ff_step(found)
    while waiting:
        ff_step(found)
    if few:
        experts += written[0]
    else:
        experts += [jnp.stack(items[::-1]).astype(f32)[:, None] for items in zip(*ff_parts)]
    matrix = ((layers, features, features), f32, whole)
    keys, values, columns, vectors, late = run(
        "assemble",
        partial(assemble_kernel, n, layers, tasks),
        1,
        [(me[None], in_smem)] + [const(a) for a in found],
        [
            matrix,
            matrix,
            ((n, layers * 2 * tasks, features), f32, whole),
            ((len(vectors), features), f32, whole),
            ((tasks * n, features), f32, whole),
        ],
        0,
        24,
    )
    columns = columns.reshape(n, layers, 2, tasks, features).transpose(2, 1, 3, 4, 0)
    late = late.reshape(tasks, n, features).transpose(0, 2, 1)
    attention_columns = jnp.concatenate([columns[0, :1] + late, columns[0, 1:]], axis=0)
    vectors = vectors.reshape(layers, 4, features).transpose(1, 0, 2)
    return (
        kept[-1][-1],
        grad,
        *(vectors[j] for j in range(4)),
        keys,
        values,
        *experts,
        attention_columns,
        columns[1],
    )


def solution(mesh):
    in_specs = (
        P("dp", "expert", None),
        P(None, "dp", "expert", None),
        P(None, "dp", "expert", None),
        P("dp"),
        P(),
        P(),
        P(),
        P(),
        P(),
        P(),
        P(None, "expert", None, None),
        P(None, "expert", None, None),
        P(None, "expert", None, None),
        P(None, "expert", None, None),
        P(),
        P(),
        P("dp", "expert", None),
    )
    out_specs = (
        P("dp", "expert", None),
        P("dp", "expert", None),
        P(),
        P(),
        P(),
        P(),
        P(),
        P(),
        P(None, "expert", None, None),
        P(None, "expert", None, None),
        P(None, "expert", None, None),
        P(None, "expert", None, None),
        P(),
        P(),
    )
    return jax.shard_map(local, mesh=mesh, in_specs=in_specs, out_specs=out_specs, check_vma=False)
```

```python
from functools import partial

import jax
import jax.numpy as jnp
from jax import lax
from jax.experimental import pallas as pl
from jax.experimental.pallas import tpu as pltpu
from jax.sharding import PartitionSpec as P

HEADS = 6
epsilon = 1e-06
f32, bf16 = jnp.float32, jnp.bfloat16
NN, NT, TN = ((1,), (0,)), ((1,), (1,)), ((0,), (0,))
MIB = 1 << 20


def mm(left, right, dims=NN, precision=None):
    return lax.dot_general(
        left, right, (dims, ((), ())), preferred_element_type=f32, precision=precision
    )


def whole(array):
    rank = len(array.shape)
    return pl.BlockSpec(array.shape, lambda i: (0,) * rank)


def per_image(array):
    rank = len(array.shape)
    return pl.BlockSpec((1,) + tuple(array.shape[1:]), lambda i: (i,) + (0,) * (rank - 1))


def per_image_after(first):
    def maker(array):
        rank = len(array.shape)
        return pl.BlockSpec(
            (1,) + tuple(array.shape[1:]), lambda i: (first + i,) + (0,) * (rank - 1)
        )

    return maker


def per_image_second(array):
    rank = len(array.shape)
    return pl.BlockSpec(
        (array.shape[0], 1) + tuple(array.shape[2:]), lambda i: (0, i) + (0,) * (rank - 2)
    )


def at_layer(layer):
    def maker(array):
        rank = len(array.shape)
        lead = rank - 2
        return pl.BlockSpec(
            (None,) * lead + tuple(array.shape[lead:]),
            lambda i: (layer,) + (0,) * (rank - 1),
        )

    return maker


def in_smem(array):
    return pl.BlockSpec(memory_space=pltpu.SMEM)


def run(name, kernel, images, ins, outs, flops, limit, scratch=()):
    shapes = [jax.ShapeDtypeStruct(shape, dtype) for shape, dtype, *_ in outs]
    moved = sum(a.size * a.dtype.itemsize for a, _ in ins)
    moved += sum(s.size * s.dtype.itemsize for s in shapes)
    out_specs = [item[2](s) for s, item in zip(shapes, outs)]
    shapes = [pltpu.HBM(*item[:2]) if len(item) > 3 else s for s, item in zip(shapes, outs)]
    return pl.pallas_call(
        kernel,
        grid=(images,),
        in_specs=[maker(a) for a, maker in ins],
        out_specs=out_specs,
        out_shape=shapes,
        scratch_shapes=list(scratch),
        compiler_params=pltpu.CompilerParams(
            dimension_semantics=("arbitrary",), vmem_limit_bytes=limit * MIB
        ),
        cost_estimate=pl.CostEstimate(flops=1, bytes_accessed=1, transcendentals=0),
        name=name,
    )(*[a for a, _ in ins])


def rows_of(refs, rows=None):
    return jnp.concatenate([r[0].astype(f32)[:rows] for r in refs], axis=0)


def home_of(refs, rows, mine):
    total = refs[0][0].astype(f32)[rows:]
    for r in refs[1:]:
        total = total + r[0].astype(f32)[rows:]
    return jnp.sum(total * mine, axis=0, keepdims=True)


def put_rows(rows, own_ref, sib_ref):
    half = own_ref.shape[0]
    size = own_ref.shape[2]
    for d in range(2 * half):
        target = own_ref if d % 2 == 0 else sib_ref
        target[d // 2, 0] = rows[d * size : (d + 1) * size].astype(bf16)


def one_hot(slot_ref, slots):
    slot = slot_ref[0]
    spots = lax.broadcasted_iota(jnp.int32, (slots, slot.shape[1]), 0)
    return spots == slot


def masked_softmax(logits, mask, axis):
    top = jnp.max(jnp.where(mask, logits, -3e38), axis=axis, keepdims=True)
    weights = jnp.where(mask, jnp.exp(jnp.minimum(logits - top, 0.0)), 0.0)
    return weights / jnp.sum(weights, axis=axis, keepdims=True)


def own_gate(rows_low, router, mask8, mine):
    gates = masked_softmax(mm(router, rows_low, NT), mask8 > 0.5, 0)
    return jnp.sum(gates * mine, axis=0, keepdims=True)


def attend_kernel(n, *refs):
    x_refs, refs = refs[:n], refs[n:]
    mask_ref, slot_ref, router_ref, mine_ref, wk, wv, wq, wo, *refs = refs
    own, sib, x_out, c_out, q_out, k_out, v_out, p_out, mixed_out, result_out, gate_out = refs
    slots, features = c_out.shape[1:]
    size = features // HEADS
    x = rows_of(x_refs).astype(bf16)
    x_out[0] = x
    hot = one_hot(slot_ref, slots)
    hot_low = hot.astype(f32).astype(bf16)
    gate_row = own_gate(x, router_ref[0], mask_ref[0], mine_ref[...])
    gate = jnp.sum(jnp.where(hot, gate_row, 0.0), axis=1, keepdims=True)
    gate_out[0] = gate
    copies = mm(hot_low, x).astype(bf16)
    c_out[0] = copies
    queries = (mm(copies, wq[...]).astype(bf16).astype(f32) * size ** (-0.5)).astype(bf16)
    q_out[0] = queries
    keys = mm(x, wk[...]).astype(bf16)
    k_out[0] = keys
    values = mm(x, wv[...])
    v_out[0] = values.astype(bf16)
    values_t = values.T.astype(bf16)
    low = lax.broadcasted_iota(jnp.int32, (slots, 2 * size), 1) < size
    zero = jnp.zeros((slots, 2 * size), bf16)
    mixed_t = []
    for head in range(HEADS):
        lanes = slice(head // 2 * 2 * size, (head // 2 + 1) * 2 * size)
        q_head = jnp.where(low if head % 2 == 0 else jnp.logical_not(low), queries[:, lanes], zero)
        scores = mm(keys[:, lanes], q_head, NT)
        weights = jnp.exp(scores - jnp.max(scores, axis=0, keepdims=True))
        inverse = 1.0 / jnp.sum(weights, axis=0, keepdims=True)
        probs = (weights * inverse).astype(bf16)
        p_out[0, head] = probs
        mixed_t.append(mm(values_t[head * size : (head + 1) * size], probs))
    mixed = jnp.concatenate(mixed_t, axis=0).T.astype(bf16)
    mixed_out[0] = mixed
    result = mm(mixed, wo[...]).astype(bf16)
    result_out[0] = result
    put_rows(mm(hot_low, (gate * result.astype(f32)).astype(bf16), TN), own, sib)


def attend_back_kernel(n, rows, *refs):
    g_refs, refs = refs[:n], refs[n:]
    me_ref, slot_ref, router_ref, mine_ref, wk, wv, wq, wo, *refs = refs
    x_ref, c_ref, q_ref, k_ref, v_ref, p_ref, mixed_ref, result_ref, gate_ref, *refs = refs
    own, sib, gr_out, dq_out, router_out, home_out, key_sum, value_sum = refs
    image = pl.program_id(0)
    slots, features = c_ref.shape[1:]
    size = features // HEADS
    hot = one_hot(slot_ref, slots)
    hot_low = hot.astype(f32).astype(bf16)
    gate = gate_ref[0]
    picked = mm(hot_low, rows_of(g_refs, rows).astype(bf16))
    home_out[0] = home_of(g_refs, rows, mine_ref[...])
    gr = (gate * picked).astype(bf16)
    gr_out[0] = gr
    turn = gate * jnp.sum(picked * result_ref[0].astype(f32), axis=1, keepdims=True)
    grad_mixed = mm(gr, wo[...], NT).astype(bf16)
    keys = k_ref[0]
    keys_t = keys.astype(f32).T.astype(bf16)
    queries = q_ref[0]
    values = v_ref[0]
    low = lax.broadcasted_iota(jnp.int32, (slots, 2 * size), 1) < size
    zero = jnp.zeros((slots, 2 * size), bf16)
    dq_t, dk, dv = [], [], []
    for head in range(HEADS):
        lanes = slice(head // 2 * 2 * size, (head // 2 + 1) * 2 * size)
        keep = low if head % 2 == 0 else jnp.logical_not(low)
        q_head = jnp.where(keep, queries[:, lanes], zero)
        gm_head = jnp.where(keep, grad_mixed[:, lanes], zero)
        probs = p_ref[0, head]
        dv_part = mm(probs, gm_head)
        probs_wide = probs.astype(f32)
        grad_probs = mm(values[:, lanes], gm_head, NT)
        inner = jnp.sum(probs_wide * grad_probs, axis=0, keepdims=True)
        grad_scores = (probs_wide * (grad_probs - inner)).astype(bf16)
        dq_t.append(mm(keys_t[head * size : (head + 1) * size], grad_scores))
        dk_part = mm(grad_scores, q_head)
        if head % 2 == 0:
            dk.append(dk_part)
            dv.append(dv_part)
        else:
            dk[-1] += dk_part
            dv[-1] += dv_part
    dq = (jnp.concatenate(dq_t, axis=0).T * size ** (-0.5)).astype(bf16)
    dq_out[0] = dq
    dk = jnp.concatenate(dk, axis=1).astype(bf16)
    dv = jnp.concatenate(dv, axis=1).astype(bf16)
    copies = c_ref[0].astype(f32)
    router_out[0] = jnp.sum(turn * copies, axis=0, keepdims=True)
    router_row = jnp.sum(mine_ref[...] * router_ref[0].astype(f32), axis=0, keepdims=True)
    back = mm(dq, wq[...], NT) + turn * router_row
    back = mm(hot_low, back.astype(bf16), TN) + mm(dk, wk[...], NT) + mm(dv, wv[...], NT)
    step = -(-rows // 16) * 16
    at = pl.ds(pl.multiple_of(image * step, 16), step)
    gap = jnp.zeros((step - rows, features), f32)
    for d in range(n):
        target = own if d % 2 == 0 else sib
        part = back[d * rows : (d + 1) * rows]
        if step > rows:
            part = jnp.concatenate([part, gap], axis=0)
        target[d // 2, at, :] = part.astype(bf16)
    key_part, value_part = mm(x_ref[0], dk, TN), mm(x_ref[0], dv, TN)

    @pl.when(image == 0)
    def _():
        key_sum[...] = key_part
        value_sum[...] = value_part

    @pl.when(image > 0)
    def _():
        key_sum[...] += key_part
        value_sum[...] += value_part

    @pl.when(image == pl.num_programs(0) - 1)
    def _():
        share = features // n
        start = own.shape[1] - 2 * share
        for d in range(n):
            target = own if d % 2 == 0 else sib
            taken = pl.ds(pl.multiple_of((me_ref[0] ^ d) * share, 8), share)
            both = jnp.concatenate([key_sum[taken, :], value_sum[taken, :]], axis=0)
            target[d // 2, start:, :] = both.astype(bf16)


def gelu_parts(hidden):
    phi = 0.5 + 0.5 * lax.erf(hidden * (0.5**0.5))
    bell = jnp.exp(-0.5 * hidden * hidden) * 0.3989422804014327
    return hidden * phi, phi + hidden * bell


def forward_body(x_refs, mask_ref, slot_ref, router_ref, mine_ref, up, down, chunk, outs):
    own, sib, c_out, slope_out, result_out, gate_out, *active_out = outs
    slots = c_out.shape[1]
    x = rows_of(x_refs).astype(bf16)
    hot = one_hot(slot_ref, slots)
    hot_low = hot.astype(f32).astype(bf16)
    gate_row = own_gate(x, router_ref[0], mask_ref[0], mine_ref[...])
    gate = jnp.sum(jnp.where(hot, gate_row, 0.0), axis=1, keepdims=True)
    gate_out[0] = gate
    copies = mm(hot_low, x).astype(bf16)
    c_out[0] = copies
    total = None
    for at in range(0, up.shape[1], chunk):
        cols = slice(at, at + chunk)
        active, slope = gelu_parts(mm(copies, up[:, cols]))
        active = active.astype(bf16)
        for r in active_out:
            r[0, :, cols] = active
        slope_out[0, :, cols] = slope.astype(bf16)
        part = mm(active, down[cols, :])
        total = part if total is None else total + part
    result = total.astype(bf16)
    result_out[0] = result
    put_rows(mm(hot_low, (gate * result.astype(f32)).astype(bf16), TN), own, sib)


def backward_body(g_refs, rows, slot_ref, router_ref, mine_ref, up, down, chunk, kept, outs):
    c_ref, slope_ref, result_ref, gate_ref = kept
    own, sib, gr_out, router_out, *gh_out = outs
    slots = c_ref.shape[1]
    hot_low = one_hot(slot_ref, slots).astype(f32).astype(bf16)
    gate = gate_ref[0]
    picked = mm(hot_low, rows_of(g_refs, rows).astype(bf16))
    gr = (gate * picked).astype(bf16)
    gr_out[0] = gr
    turn = gate * jnp.sum(picked * result_ref[0].astype(f32), axis=1, keepdims=True)
    total = None
    for at in range(0, up.shape[1], chunk):
        cols = slice(at, at + chunk)
        gh = (mm(gr, down[cols, :], NT) * slope_ref[0, :, cols].astype(f32)).astype(bf16)
        for r in gh_out:
            r[0, :, cols] = gh
        part = mm(gh, up[:, cols], NT)
        total = part if total is None else total + part
    router_out[0] = jnp.sum(turn * c_ref[0].astype(f32), axis=0, keepdims=True)
    router_row = jnp.sum(mine_ref[...] * router_ref[0].astype(f32), axis=0, keepdims=True)
    back = total + turn * router_row
    put_rows(mm(hot_low, back.astype(bf16), TN), own, sib)


def perceptron_kernel(n, chunk, *refs):
    x_refs, refs = refs[:n], refs[n:]
    mask_ref, slot_ref, router_ref, mine_ref, up, down, *outs = refs
    forward_body(x_refs, mask_ref, slot_ref, router_ref, mine_ref, up, down, chunk, outs)


def perceptron_back_kernel(n, rows, chunk, *refs):
    g_refs, refs = refs[:n], refs[n:]
    slot_ref, router_ref, mine_ref, up, down, c_ref, slope, result, gate, *outs = refs
    if g_refs[0].shape[1] > rows:
        home_out, *outs = outs
        home_out[0] = home_of(g_refs, rows, mine_ref[...])
    kept = (c_ref, slope, result, gate)
    backward_body(g_refs, rows, slot_ref, router_ref, mine_ref, up, down, chunk, kept, outs)


def ff_gradient_kernel(sides, given, *refs):
    side_refs, (up, down, *refs) = refs[:sides], refs[sides:]
    up_out, down_out = refs[given:]
    features = up.shape[0]
    copies, gr = (r[...].reshape(-1, features) for r in side_refs)
    active, slope = gelu_parts(mm(up[...], copies, ((0,), (1,))))
    gh = (mm(down[...], gr, NT) * slope).astype(bf16)
    up_out[...] = mm(gh, copies).T
    down_out[...] = mm(active.astype(bf16), gr)


def ff_gradient(sides, up, down, layer, width, start, steps, before):
    features = up.shape[2]
    given, count = len(before), len(sides)
    shapes = [jax.ShapeDtypeStruct(a.shape, f32) for a in (up, down)]
    specs = [
        pl.BlockSpec((None, None, features, width), lambda j: (layer, 0, 0, start + j)),
        pl.BlockSpec((None, None, width, features), lambda j: (layer, 0, start + j, 0)),
    ]
    return pl.pallas_call(
        partial(ff_gradient_kernel, count, given),
        grid=(steps,),
        in_specs=[whole(a) for a in sides]
        + specs
        + [pl.BlockSpec(memory_space=pl.ANY)] * given,
        out_specs=specs,
        out_shape=shapes,
        input_output_aliases={count + 2 + j: j for j in range(given)},
        compiler_params=pltpu.CompilerParams(
            dimension_semantics=("arbitrary",), vmem_limit_bytes=60 * MIB
        ),
        cost_estimate=pl.CostEstimate(flops=1, bytes_accessed=1, transcendentals=0),
        name="ff_gradient",
    )(*sides, up, down, *before)


def assemble_kernel(n, layers, tasks, me_ref, *refs):
    found, (key_out, value_out, column_out, vector_out, late_out) = refs[:n], refs[n:]
    share = key_out.shape[1] // n
    columns, vectors, late = column_out.shape[1], vector_out.shape[0], late_out.shape[0]
    at = layers * 2 * share
    vector_sum = late_sum = 0.0
    for d in range(n):
        place = me_ref[0] ^ d
        held = found[d][...].astype(f32)
        rows = pl.ds(pl.multiple_of(place * share, 8), share)
        for layer in range(layers):
            key_out[layer, rows, :] = held[2 * layer * share : (2 * layer + 1) * share]
            value_out[layer, rows, :] = held[(2 * layer + 1) * share : (2 * layer + 2) * share]
        late_sum = late_sum + held[at : at + late]
        vector_sum = vector_sum + held[at + late : at + late + vectors]
        column_out[place] = held[at + late + vectors : at + late + vectors + columns]
    vector_out[...] = vector_sum
    late_out[...] = late_sum


def flat(ref):
    images, rows, features = ref.shape
    return ref[...].astype(f32).reshape(images * rows, features)


def normed(state):
    centered = state - jnp.mean(state, axis=-1, keepdims=True)
    inverse = lax.rsqrt(jnp.mean(centered * centered, axis=-1, keepdims=True) + epsilon)
    return centered * inverse, inverse


def enter_kernel(state_ref, gain_ref, shift_ref, extra_ref, named_ref, low_out, sent_out):
    unit, _ = normed(flat(state_ref))
    low = (unit * gain_ref[...] + shift_ref[...]).reshape(low_out.shape).astype(bf16)
    low_out[...] = low
    images = low.shape[0]
    for i in range(images):
        sent_out[i] = low[i]
        sent_out[images + i] = extra_ref[i]
    sent_out[2 * images] = named_ref[...]


def join_kernel(parts, last, *refs):
    part_refs, refs = refs[:parts], refs[parts:]
    state_ref, gain_ref, shift_ref, state_out, *low_out = refs
    state = flat(state_ref)
    added = flat(part_refs[0])
    for r in part_refs[1:]:
        added = added + flat(r)
    state = state + added
    state_out[...] = state.reshape(state_out.shape)
    if not last:
        unit, _ = normed(state)
        rows = unit * gain_ref[...] + shift_ref[...]
        low_out[0][...] = rows.reshape(low_out[0].shape).astype(bf16)


def join_back_kernel(parts, *refs):
    part_refs, refs = refs[:parts], refs[parts:]
    grad_ref, before_ref, after_ref, low_ref, router_ref, mask_ref, gain_ref, *refs = refs
    grad_out, low_out, gain_out, shift_out, *more = refs
    images, rows, features = grad_ref.shape
    total = part_refs[0][...].astype(f32)
    for r in part_refs[1:]:
        total = total + r[...].astype(f32)
    if total.ndim == 3:
        (home_out,) = more
        back = total.reshape(images * rows, features)
    else:
        home_out, share_out = more
        step = -(-rows // 16) * 16
        back = jnp.concatenate([total[i * step : i * step + rows] for i in range(images)], axis=0)
        share_out[...] = total[images * step :].astype(bf16)
    grad = flat(grad_ref)
    before = flat(before_ref)
    share = jnp.sum(grad * (flat(after_ref) - before), axis=1, keepdims=True)
    highest = lax.Precision.HIGHEST
    taken, homes = [], []
    for i in range(images):
        router = router_ref[i]
        gates = masked_softmax(mm(low_ref[i], router, NT), mask_ref[i] > 0.5, 1)
        weighted = gates * share[i * rows : (i + 1) * rows]
        taken.append(mm(weighted, router.astype(f32), NN, highest))
        homes.append(-mm(weighted, low_ref[i].astype(f32), TN, highest))
        home_out[i] = homes[-1]
    back = back - jnp.concatenate(taken, axis=0)
    unit, inverse = normed(before)
    gain_out[...] = jnp.sum(back * unit, axis=0, keepdims=True)
    shift_out[...] = jnp.sum(back, axis=0, keepdims=True)
    back = back * gain_ref[...]
    back = back - jnp.mean(back, axis=1, keepdims=True)
    back = back - unit * jnp.mean(back * unit, axis=1, keepdims=True)
    grad = grad + inverse * back
    grad_out[...] = grad.reshape(grad_out.shape)
    for i in range(images):
        sent = jnp.concatenate([grad[i * rows : (i + 1) * rows], homes[i]], axis=0)
        low_out[i] = sent.astype(bf16)


def pair(array, offset):
    size = lax.axis_size("expert")
    return lax.ppermute(array, "expert", [(i, i ^ offset) for i in range(size)])


def gather(array, beside=None):
    size = lax.axis_size("expert")
    found = {0: array}
    for d in range(size - 2, 0, -2):
        found[d] = pair(array, d)
    if beside is not None:
        arrived = [found[d] for d in range(2, size, 2)]
        beside(arrived)
        found.update(zip(range(2, size, 2), arrived))
    for d in range(0, size, 2):
        found[d + 1] = pair(found[d], 1)
    return [found[d] for d in range(size)]


def scatter(own, sib, later=None):
    other = pair(sib, 1)
    sums = [add_low(own[j], other[j]) for j in range(own.shape[0])]
    if later:
        *sums, later[-1] = lax.optimization_barrier((*sums, later[-1]))
    return [v if j == 0 else pair(v, 2 * j) for j, v in enumerate(sums)]


def add_low(left, right):
    return (left.astype(f32) + right.astype(f32)).astype(bf16)


def dp_pair(array, offset):
    size = lax.axis_size("dp")
    return lax.ppermute(array, "dp", [(i, i ^ offset) for i in range(size)])


def dp_add(array, beside):
    size = lax.axis_size("dp")
    if size & (size - 1):
        return lax.psum(array, "dp")
    offset = 1
    while offset < size:
        arrived = [dp_pair(array, offset)]
        offset *= 2
        beside(arrived, 2 if offset >= size else 1)
        array = add_low(array, arrived[0])
    return array


def local(
    inputs,
    attention_routes,
    perceptron_routes,
    task_index,
    attention_gain,
    attention_shift,
    perceptron_gain,
    perceptron_shift,
    key_weight,
    value_weight,
    query_weight,
    output_weight,
    up_weight,
    down_weight,
    attention_router,
    perceptron_router,
    cotangent,
):
    n = lax.axis_size("expert")
    me = lax.axis_index("expert").astype(jnp.int32)
    me_dp = lax.axis_index("dp").astype(jnp.int32)[None]
    dp = lax.axis_size("dp")
    images, rows, features = inputs.shape
    layers = key_weight.shape[0]
    hidden = up_weight.shape[-1]
    few = dp & (dp - 1) == 0 and dp <= 4 and features % (16 * dp) == 0
    copies_all, gr_all = {}, {}
    top = attention_routes.shape[-1]
    tasks = attention_router.shape[1]
    capacity = min(rows, rows * top // n * 4 // 3)
    slots = n * capacity
    total = n * rows
    chunk = 384
    width = 256
    mine = (jnp.arange(n, dtype=jnp.int32) == me).astype(f32)[:, None]

    routes = jnp.stack([attention_routes, perceptron_routes])
    named = (routes[..., None] == jnp.arange(n, dtype=jnp.int32)).any(axis=-2)
    home_mask = named.astype(f32)
    plane = named.astype(bf16).transpose(3, 0, 1, 2, 4).reshape(rows, -1)
    marks = plane.shape[1]
    plane = jnp.pad(plane, ((0, 0), (0, features - marks)))
    state = inputs.astype(f32)
    low, sent = run(
        "enter",
        enter_kernel,
        1,
        [
            (a, whole)
            for a in (inputs, attention_gain[:1], attention_shift[:1], cotangent, plane)
        ],
        [((images, rows, features), bf16, whole), ((2 * images + 1, rows, features), bf16, whole)],
        10**6,
        16,
    )
    x_all = gather(sent)
    cotangent_all = [(a, per_image_after(images)) for a in x_all]
    all_masks = jnp.stack([a[2 * images, :, :marks] for a in x_all])
    all_masks = all_masks.reshape(n, rows, 2, layers, images, n).transpose(2, 3, 4, 5, 0, 1)
    all_masks = all_masks.reshape(2, layers, images, n, total)
    mine_mask = jnp.einsum(
        "kliet,e->klit", all_masks, mine[:, 0].astype(bf16), preferred_element_type=f32
    )
    blocks = mine_mask.reshape(2, layers, images, n, rows)
    earlier = jnp.tril(jnp.ones((rows, rows), bf16), -1)
    position = jnp.einsum(
        "klibr,qr->klibq", blocks.astype(bf16), earlier, preferred_element_type=f32
    )
    position = position.astype(jnp.int32) + jnp.arange(n, dtype=jnp.int32)[:, None] * capacity
    slot = jnp.where(blocks > 0.5, position, -1).reshape(2, layers, images, 1, total)
    masks = all_masks.astype(f32)
    routers = (
        attention_router[:, task_index].transpose(0, 1, 3, 2),
        perceptron_router[:, task_index].transpose(0, 1, 3, 2),
    )

    row_shape = (images, rows, features)
    part_shape = (n // 2, images, rows, features)
    slot_shape = (images, slots, features)
    all_shape = (images, total, features)
    gate_shape = (images, slots, 1)
    wide_shape = (images, slots, hidden)
    probs_shape = (images, HEADS, total, slots)
    router_shape = (images, 1, features)
    part_rows = features // n
    step = -(-rows // 16) * 16
    back_shape = (n // 2, images * step + 2 * part_rows, features)
    partial_rows = (part_shape, bf16, per_image_second)
    slot_rows = (slot_shape, bf16, per_image, "hbm")
    all_rows = (all_shape, bf16, per_image, "hbm")
    wide_rows = (wide_shape, bf16, per_image, "hbm")
    gate_rows = (gate_shape, f32, per_image, "hbm")
    wide_kept = [] if few else [wide_rows]
    router_rows = (router_shape, f32, per_image)
    flop_small = 2 * images * slots * features * features
    flop_core = 2 * images * slots * total * features
    flop_wide = 2 * images * slots * features * hidden

    def image(array):
        return (array, per_image)

    def const(array):
        return (array, whole)

    def join(parts, state, gain, shift):
        last = gain is None
        if last:
            gain = shift = jnp.zeros((1, features), f32)
        outs = [(row_shape, f32, whole)] + ([] if last else [(row_shape, bf16, whole)])
        ins = [const(a) for a in (*parts, state, gain, shift)]
        return run("join", partial(join_kernel, len(parts), last), 1, ins, outs, 10**6, 16)

    def join_back(parts, grad, before, after, low, router, mask, gain):
        ins = [const(a) for a in (*parts, grad, before, after, low, router, mask, gain)]
        outs = [
            (row_shape, f32, whole),
            ((images, rows + n, features), bf16, whole),
            ((1, features), f32, whole),
            ((1, features), f32, whole),
            ((images, n, features), f32, whole),
        ]
        if parts[0].ndim == 2:
            outs.append(((2 * part_rows, features), bf16, whole))
        return run("join_back", partial(join_back_kernel, len(parts)), 1, ins, outs, 10**6, 16)

    kept = []
    for l in range(layers):
        weights = [key_weight, value_weight, query_weight, output_weight]
        own, sib, *saved = run(
            "attend",
            partial(attend_kernel, n),
            images,
            [image(a) for a in x_all]
            + [image(masks[0, l]), image(slot[0, l]), image(routers[0][l]), const(mine)]
            + [(w, at_layer(l)) for w in weights],
            [partial_rows, partial_rows, all_rows, slot_rows, slot_rows, all_rows, all_rows]
            + [(probs_shape, bf16, per_image, "hbm"), slot_rows, slot_rows, gate_rows],
            2 * flop_core + 6 * flop_small,
            60,
        )
        low_a = low
        middle, low = join(
            scatter(own, sib), state, perceptron_gain[l : l + 1], perceptron_shift[l : l + 1]
        )
        x_all = gather(low)
        ff_weights = [up_weight, down_weight]
        route_ins = [image(masks[1, l]), image(slot[1, l]), image(routers[1][l]), const(mine)]
        last = l == layers - 1
        if last:
            for j in copies_all:
                x_all[-1], copies_all[j] = lax.optimization_barrier((x_all[-1], copies_all[j]))
        own, sib, copies, slope, result, gate, *active = run(
            "perceptron",
            partial(perceptron_kernel, n, chunk),
            images,
            [image(a) for a in x_all] + route_ins + [(w, at_layer(l)) for w in ff_weights],
            [partial_rows, partial_rows, slot_rows, wide_rows, slot_rows, gate_rows] + wide_kept,
            2 * flop_wide,
            60,
        )
        kept_ff = (copies, slope, result, gate)
        if few:
            copies_all[l] = lax.all_gather(copies, "dp", axis=0, tiled=False)
        parts = scatter(own, sib)
        if last:
            (after,) = join(parts, middle, None, None)
            low_next = None
        else:
            after, low_next = join(
                parts, middle, attention_gain[l + 1 : l + 2], attention_shift[l + 1 : l + 2]
            )
        kept.append((state, low_a, saved, middle, low, copies, active, kept_ff, after))
        state = after
        low = low_next
        if not last:
            x_all = gather(low)

    grad = cotangent.astype(f32)
    grad_low = None
    gains, columns, shares, ff_parts, qo_parts = [], [], [], [], []
    steps = hidden // width
    halves = ((0, steps // 2), (steps // 2, steps - steps // 2))
    waiting = [(l, *half) for l in range(layers) for half in halves[::-1]] if few else []
    written = [()]

    def ff_step(arrived, times=1):
        for l, start, count in [waiting.pop() for _ in range(times) if waiting]:
            written[0] = ff_gradient(
                [copies_all[l], gr_all[l]],
                up_weight,
                down_weight,
                l,
                width,
                start,
                count,
                written[0],
            )
        if few:
            arrived[-1], written[0] = lax.optimization_barrier((arrived[-1], written[0]))
    for l in range(layers - 1, -1, -1):
        state, low_a, saved, middle, low_m, copies, active, kept_ff, after = kept[l]
        ff_weights = [up_weight, down_weight]
        last = l == layers - 1
        g_all = cotangent_all if last else [image(a) for a in gather(grad_low)]
        outs = run(
            "perceptron_back",
            partial(perceptron_back_kernel, n, rows, chunk),
            images,
            g_all
            + [image(slot[1, l]), image(routers[1][l]), const(mine)]
            + [(w, at_layer(l)) for w in ff_weights]
            + [image(a) for a in kept_ff],
            [router_rows] * (not last)
            + [partial_rows, partial_rows, slot_rows, router_rows]
            + wide_kept,
            2 * flop_wide,
            60,
        )
        if not last:
            columns[-1] = columns[-1] + outs[0]
            outs = outs[1:]
        own, sib, gr, router_m, *gh = outs
        parts = scatter(own, sib)
        if few:
            gr_all[l] = lax.all_gather(gr, "dp", axis=0, tiled=False)
            if not last:
                parts[-1], copies_all[l + 1], gr_all[l + 1] = lax.optimization_barrier(
                    (parts[-1], copies_all[l + 1], gr_all[l + 1])
                )
        else:
            up_part = jnp.einsum("isd,isf->df", copies, gh[0], preferred_element_type=f32)
            down_part = jnp.einsum("isf,isd->fd", active[0], gr, preferred_element_type=f32)
            both = (up_part.astype(bf16), down_part.astype(bf16))
            ff_parts.append(lax.psum(both, "dp"))
        grad, grad_low, gain_m, shift_m, _ = join_back(
            parts,
            grad,
            middle,
            after,
            low_m,
            routers[1][l],
            home_mask[1, l],
            perceptron_gain[l : l + 1],
        )
        columns.append(router_m)
        g_all = gather(grad_low)
        x, copies, queries, keys, values, probs, mixed, result, gate = saved
        weights = [key_weight, value_weight, query_weight, output_weight]
        own, sib, gr_a, dq, router_a, home = run(
            "attend_back",
            partial(attend_back_kernel, n, rows),
            images,
            [image(a) for a in g_all]
            + [(me[None], in_smem)]
            + [image(slot[0, l]), image(routers[0][l]), const(mine)]
            + [(w, at_layer(l)) for w in weights]
            + [image(a) for a in (x, copies, queries, keys, values, probs, mixed, result, gate)],
            [(back_shape, bf16, whole), (back_shape, bf16, whole)]
            + [slot_rows, slot_rows, router_rows, router_rows],
            4 * flop_core + 14 * flop_small,
            60,
            [pltpu.VMEM((features, features), f32)] * 2,
        )
        columns[-1] = columns[-1] + home
        columns.append(router_a)
        later = [gr_all[layers - 1]] if few and l == 0 < layers - 1 else []
        parts = scatter(own, sib, later)
        if later:
            gr_all[layers - 1] = later[0]
        both = (
            jnp.einsum("isd,isf->df", copies, dq, preferred_element_type=f32).astype(bf16),
            jnp.einsum("isf,isd->fd", mixed, gr_a, preferred_element_type=f32).astype(bf16),
        )
        parts[-1], *both = lax.optimization_barrier((parts[-1], *both))
        qo_parts.append(both)
        if few and l < layers - 1:
            parts[-1], gr_all[l] = lax.optimization_barrier((parts[-1], gr_all[l]))
            if l == 0:
                ff_step(parts)
        grad, grad_low, gain_a, shift_a, late, share = join_back(
            parts,
            grad,
            state,
            middle,
            low_a,
            routers[0][l],
            home_mask[0, l],
            attention_gain[l : l + 1],
        )
        gains.append((gain_a, shift_a, gain_m, shift_m))
        shares.append(share)

    if few:
        qo_parts, gr_all[0] = lax.optimization_barrier((qo_parts, gr_all[0]))

    experts = list(zip(*lax.psum(qo_parts, "dp")))
    picked = (task_index[:, None] == jnp.arange(tasks, dtype=jnp.int32)[None, :]).astype(f32)
    highest = lax.Precision.HIGHEST
    columns = jnp.stack([c[:, 0] for c in columns[::-1]])
    columns = jnp.einsum("it,lid->ltd", picked, columns, precision=highest)
    late = jnp.einsum("it,ied->ted", picked, late, precision=highest)
    vectors = [v for items in gains[::-1] for v in items]
    payload = [
        *shares[::-1],
        late.reshape(tasks * n, features).astype(bf16),
        *[v.astype(bf16) for v in vectors],
        columns.reshape(layers * 2 * tasks, features).astype(bf16),
    ]
    used = sum(p.shape[0] for p in payload)
    payload.append(jnp.zeros((-used % 16, features), bf16))
    shared = dp_add(jnp.concatenate(payload, axis=0), ff_step)

    def reduced(arrived):
        nonlocal experts
        arrived[-1], experts = lax.optimization_barrier((arrived[-1], experts))

    found = gather(shared, reduced)
    while waiting:
        ff_step(found)
    experts = [jnp.stack(items[::-1]).astype(f32)[:, None] for items in experts]
    if few:
        experts += written[0]
    else:
        experts += [jnp.stack(items[::-1]).astype(f32)[:, None] for items in zip(*ff_parts)]
    matrix = ((layers, features, features), f32, whole)
    keys, values, columns, vectors, late = run(
        "assemble",
        partial(assemble_kernel, n, layers, tasks),
        1,
        [(me[None], in_smem)] + [const(a) for a in found],
        [
            matrix,
            matrix,
            ((n, layers * 2 * tasks, features), f32, whole),
            ((len(vectors), features), f32, whole),
            ((tasks * n, features), f32, whole),
        ],
        0,
        24,
    )
    columns = columns.reshape(n, layers, 2, tasks, features).transpose(2, 1, 3, 4, 0)
    late = late.reshape(tasks, n, features).transpose(0, 2, 1)
    attention_columns = jnp.concatenate([columns[0, :1] + late, columns[0, 1:]], axis=0)
    vectors = vectors.reshape(layers, 4, features).transpose(1, 0, 2)
    return (
        kept[-1][-1],
        grad,
        *(vectors[j] for j in range(4)),
        keys,
        values,
        *experts,
        attention_columns,
        columns[1],
    )


def solution(mesh):
    in_specs = (
        P("dp", "expert", None),
        P(None, "dp", "expert", None),
        P(None, "dp", "expert", None),
        P("dp"),
        P(),
        P(),
        P(),
        P(),
        P(),
        P(),
        P(None, "expert", None, None),
        P(None, "expert", None, None),
        P(None, "expert", None, None),
        P(None, "expert", None, None),
        P(),
        P(),
        P("dp", "expert", None),
    )
    out_specs = (
        P("dp", "expert", None),
        P("dp", "expert", None),
        P(),
        P(),
        P(),
        P(),
        P(),
        P(),
        P(None, "expert", None, None),
        P(None, "expert", None, None),
        P(None, "expert", None, None),
        P(None, "expert", None, None),
        P(),
        P(),
    )
    return jax.shard_map(local, mesh=mesh, in_specs=in_specs, out_specs=out_specs, check_vma=False)
```

```python
from functools import partial

import jax
import jax.numpy as jnp
from jax import lax
from jax.experimental import pallas as pl
from jax.experimental.pallas import tpu as pltpu
from jax.sharding import PartitionSpec as P

HEADS = 6
epsilon = 1e-06
f32, bf16 = jnp.float32, jnp.bfloat16
NN, NT, TN = ((1,), (0,)), ((1,), (1,)), ((0,), (0,))
MIB = 1 << 20


def mm(left, right, dims=NN, precision=None):
    return lax.dot_general(
        left, right, (dims, ((), ())), preferred_element_type=f32, precision=precision
    )


def whole(array):
    rank = len(array.shape)
    return pl.BlockSpec(array.shape, lambda i: (0,) * rank)


def per_image(array):
    rank = len(array.shape)
    return pl.BlockSpec((1,) + tuple(array.shape[1:]), lambda i: (i,) + (0,) * (rank - 1))


def per_image_after(first):
    def maker(array):
        rank = len(array.shape)
        return pl.BlockSpec(
            (1,) + tuple(array.shape[1:]), lambda i: (first + i,) + (0,) * (rank - 1)
        )

    return maker


def per_image_second(array):
    rank = len(array.shape)
    return pl.BlockSpec(
        (array.shape[0], 1) + tuple(array.shape[2:]), lambda i: (0, i) + (0,) * (rank - 2)
    )


def at_set(*lead):
    def maker(array):
        rank = len(array.shape)
        count = len(lead)
        return pl.BlockSpec(
            (None,) * count + (1,) + tuple(array.shape[count + 1 :]),
            lambda i: (*lead, i) + (0,) * (rank - count - 1),
        )

    return maker


def set_whole(*lead):
    def maker(array):
        rank, count = len(array.shape), len(lead)
        return pl.BlockSpec(
            (None,) * count + tuple(array.shape[count:]),
            lambda i: (*lead,) + (0,) * (rank - count),
        )

    return maker


def at_layer(layer):
    def maker(array):
        rank = len(array.shape)
        lead = rank - 2
        return pl.BlockSpec(
            (None,) * lead + tuple(array.shape[lead:]),
            lambda i: (layer,) + (0,) * (rank - 1),
        )

    return maker


def in_smem(array):
    return pl.BlockSpec(memory_space=pltpu.SMEM)


def run(name, kernel, images, ins, outs, flops, limit, scratch=()):
    ins = [
        (pltpu.with_memory_space_constraint(a, pltpu.HBM) if pinned else a, maker)
        for a, maker, *pinned in ins
    ]
    shapes = [jax.ShapeDtypeStruct(shape, dtype) for shape, dtype, *_ in outs]
    moved = sum(a.size * a.dtype.itemsize for a, _ in ins)
    moved += sum(s.size * s.dtype.itemsize for s in shapes)
    out_specs = [item[2](s) for s, item in zip(shapes, outs)]
    shapes = [pltpu.HBM(*item[:2]) if len(item) > 3 else s for s, item in zip(shapes, outs)]
    return pl.pallas_call(
        kernel,
        grid=(images,),
        in_specs=[maker(a) for a, maker in ins],
        out_specs=out_specs,
        out_shape=shapes,
        scratch_shapes=list(scratch),
        compiler_params=pltpu.CompilerParams(
            dimension_semantics=("arbitrary",), vmem_limit_bytes=limit * MIB
        ),
        cost_estimate=pl.CostEstimate(flops=1, bytes_accessed=1, transcendentals=0),
        name=name,
    )(*[a for a, _ in ins])


def rows_of(refs, rows=None):
    return jnp.concatenate([r[0].astype(f32)[:rows] for r in refs], axis=0)


def home_of(refs, rows, mine):
    total = refs[0][0].astype(f32)[rows:]
    for r in refs[1:]:
        total = total + r[0].astype(f32)[rows:]
    return jnp.sum(total * mine, axis=0, keepdims=True)


def put_rows(rows, own_ref, sib_ref):
    half = own_ref.shape[0]
    size = own_ref.shape[2]
    for d in range(2 * half):
        target = own_ref if d % 2 == 0 else sib_ref
        target[d // 2, 0] = rows[d * size : (d + 1) * size].astype(bf16)


def one_hot(slot_ref, slots):
    slot = slot_ref[0]
    spots = lax.broadcasted_iota(jnp.int32, (slots, slot.shape[1]), 0)
    return spots == slot


def masked_softmax(logits, mask, axis):
    top = jnp.max(jnp.where(mask, logits, -3e38), axis=axis, keepdims=True)
    weights = jnp.where(mask, jnp.exp(jnp.minimum(logits - top, 0.0)), 0.0)
    return weights / jnp.sum(weights, axis=axis, keepdims=True)


def own_gate(rows_low, router, mask8, mine):
    gates = masked_softmax(mm(router, rows_low, NT), mask8 > 0.5, 0)
    return jnp.sum(gates * mine, axis=0, keepdims=True)


def attend_kernel(n, *refs):
    x_refs, refs = refs[:n], refs[n:]
    mask_ref, slot_ref, router_ref, mine_ref, wk, wv, wq, wo, *refs = refs
    own, sib, x_out, c_out, q_out, k_out, v_out, p_out, mixed_out, *refs = refs
    result_out, gate_out, values_t, mixed_t = refs
    slots, features = c_out.shape[1:]
    size = features // HEADS
    x = rows_of(x_refs).astype(bf16)
    x_out[0] = x
    hot = one_hot(slot_ref, slots)
    hot_low = hot.astype(f32).astype(bf16)
    gate_row = own_gate(x, router_ref[0], mask_ref[0], mine_ref[...])
    gate = jnp.sum(jnp.where(hot, gate_row, 0.0), axis=1, keepdims=True)
    gate_out[0] = gate
    copies = mm(hot_low, x).astype(bf16)
    c_out[0] = copies
    queries = (mm(copies, wq[...]).astype(bf16).astype(f32) * size ** (-0.5)).astype(bf16)
    q_out[0] = queries
    keys = mm(x, wk[...]).astype(bf16)
    k_out[0] = keys
    values = mm(x, wv[...])
    v_out[0] = values.astype(bf16)
    values_t[...] = values.T.astype(bf16)
    low = lax.broadcasted_iota(jnp.int32, (slots, 2 * size), 1) < size
    zero = jnp.zeros((slots, 2 * size), bf16)

    def two_heads(pair_index, carry):
        start = pl.multiple_of(pair_index * 2 * size, 2 * size)
        lanes = pl.ds(start, 2 * size)
        for half in range(2):
            keep = low if half == 0 else jnp.logical_not(low)
            scores = mm(k_out[0, :, lanes], jnp.where(keep, q_out[0, :, lanes], zero), NT)
            weights = jnp.exp(scores - jnp.max(scores, axis=0, keepdims=True))
            inverse = 1.0 / jnp.sum(weights, axis=0, keepdims=True)
            probs = (weights * inverse).astype(bf16)
            p_out[0, 2 * pair_index + half] = probs
            rows = pl.ds(pl.multiple_of(start + half * size, size), size)
            mixed_t[rows, :] = mm(values_t[rows, :], probs)
        return carry

    lax.fori_loop(0, HEADS // 2, two_heads, 0, unroll=True)
    mixed = mixed_t[...].T.astype(bf16)
    mixed_out[0] = mixed
    result = mm(mixed, wo[...]).astype(bf16)
    result_out[0] = result
    put_rows(mm(hot_low, (gate * result.astype(f32)).astype(bf16), TN), own, sib)


def attend_back_kernel(n, rows, *refs):
    g_refs, refs = refs[:n], refs[n:]
    me_ref, slot_ref, router_ref, mine_ref, wk, wv, wq, wo, *refs = refs
    x_ref, c_ref, q_ref, k_ref, v_ref, p_ref, mixed_ref, result_ref, gate_ref, *refs = refs
    own, sib, gr_out, dq_out, router_out, home_out, key_sum, value_sum, *refs = refs
    grad_mixed, keys_t, dq_t, dk_wide, dv_wide = refs
    image = pl.program_id(0)
    slots, features = c_ref.shape[1:]
    size = features // HEADS
    hot = one_hot(slot_ref, slots)
    hot_low = hot.astype(f32).astype(bf16)
    gate = gate_ref[0]
    picked = mm(hot_low, rows_of(g_refs, rows).astype(bf16))
    home_out[0] = home_of(g_refs, rows, mine_ref[...])
    gr = (gate * picked).astype(bf16)
    gr_out[0] = gr
    turn = gate * jnp.sum(picked * result_ref[0].astype(f32), axis=1, keepdims=True)
    grad_mixed[...] = mm(gr, wo[...], NT).astype(bf16)
    keys_t[...] = k_ref[0].astype(f32).T.astype(bf16)
    low = lax.broadcasted_iota(jnp.int32, (slots, 2 * size), 1) < size
    zero = jnp.zeros((slots, 2 * size), bf16)

    def two_heads(pair_index, carry):
        start = pl.multiple_of(pair_index * 2 * size, 2 * size)
        lanes = pl.ds(start, 2 * size)
        dk_part = dv_part = 0.0
        for half in range(2):
            keep = low if half == 0 else jnp.logical_not(low)
            q_head = jnp.where(keep, q_ref[0, :, lanes], zero)
            gm_head = jnp.where(keep, grad_mixed[:, lanes], zero)
            probs = p_ref[0, 2 * pair_index + half]
            dv_part = dv_part + mm(probs, gm_head)
            probs_wide = probs.astype(f32)
            grad_probs = mm(v_ref[0, :, lanes], gm_head, NT)
            inner = jnp.sum(probs_wide * grad_probs, axis=0, keepdims=True)
            grad_scores = (probs_wide * (grad_probs - inner)).astype(bf16)
            rows = pl.ds(pl.multiple_of(start + half * size, size), size)
            dq_t[rows, :] = mm(keys_t[rows, :], grad_scores)
            dk_part = dk_part + mm(grad_scores, q_head)
        dk_wide[:, lanes] = dk_part.astype(bf16)
        dv_wide[:, lanes] = dv_part.astype(bf16)
        return carry

    lax.fori_loop(0, HEADS // 2, two_heads, 0)
    dq = (dq_t[...].T * size ** (-0.5)).astype(bf16)
    dq_out[0] = dq
    dk, dv = dk_wide[...], dv_wide[...]
    copies = c_ref[0].astype(f32)
    router_out[0] = jnp.sum(turn * copies, axis=0, keepdims=True)
    router_row = jnp.sum(mine_ref[...] * router_ref[0].astype(f32), axis=0, keepdims=True)
    back = mm(dq, wq[...], NT) + turn * router_row
    back = mm(hot_low, back.astype(bf16), TN) + mm(dk, wk[...], NT) + mm(dv, wv[...], NT)
    step = -(-rows // 16) * 16
    at = pl.ds(pl.multiple_of(image * step, 16), step)
    gap = jnp.zeros((step - rows, features), f32)
    for d in range(n):
        target = own if d % 2 == 0 else sib
        part = back[d * rows : (d + 1) * rows]
        if step > rows:
            part = jnp.concatenate([part, gap], axis=0)
        target[d // 2, at, :] = part.astype(bf16)
    key_part, value_part = mm(x_ref[0], dk, TN), mm(x_ref[0], dv, TN)

    @pl.when(image == 0)
    def _():
        key_sum[...] = key_part
        value_sum[...] = value_part

    @pl.when(image > 0)
    def _():
        key_sum[...] += key_part
        value_sum[...] += value_part

    @pl.when(image == pl.num_programs(0) - 1)
    def _():
        share = features // n
        start = own.shape[1] - 2 * share
        for d in range(n):
            target = own if d % 2 == 0 else sib
            taken = pl.ds(pl.multiple_of((me_ref[0] ^ d) * share, 8), share)
            both = jnp.concatenate([key_sum[taken, :], value_sum[taken, :]], axis=0)
            target[d // 2, start:, :] = both.astype(bf16)


def gelu_parts(hidden):
    phi = 0.5 + 0.5 * lax.erf(hidden * (0.5**0.5))
    bell = jnp.exp(-0.5 * hidden * hidden) * 0.3989422804014327
    return hidden * phi, phi + hidden * bell


def forward_body(x_refs, mask_ref, slot_ref, router_ref, mine_ref, up, down, chunk, outs):
    own, sib, c_out, slope_out, result_out, gate_out, *active_out = outs
    slots = c_out.shape[1]
    x = rows_of(x_refs).astype(bf16)
    hot = one_hot(slot_ref, slots)
    hot_low = hot.astype(f32).astype(bf16)
    gate_row = own_gate(x, router_ref[0], mask_ref[0], mine_ref[...])
    gate = jnp.sum(jnp.where(hot, gate_row, 0.0), axis=1, keepdims=True)
    gate_out[0] = gate
    copies = mm(hot_low, x).astype(bf16)
    c_out[0] = copies
    total = None
    for at in range(0, up.shape[1], chunk):
        cols = slice(at, at + chunk)
        active, slope = gelu_parts(mm(copies, up[:, cols]))
        active = active.astype(bf16)
        for r in active_out:
            r[0, :, cols] = active
        slope_out[0, :, cols] = slope.astype(bf16)
        part = mm(active, down[cols, :])
        total = part if total is None else total + part
    result = total.astype(bf16)
    result_out[0] = result
    put_rows(mm(hot_low, (gate * result.astype(f32)).astype(bf16), TN), own, sib)


def backward_body(g_refs, rows, slot_ref, router_ref, mine_ref, up, down, chunk, kept, outs):
    c_ref, slope_ref, result_ref, gate_ref = kept
    own, sib, gr_out, router_out, *gh_out = outs
    slots = c_ref.shape[1]
    hot_low = one_hot(slot_ref, slots).astype(f32).astype(bf16)
    gate = gate_ref[0]
    picked = mm(hot_low, rows_of(g_refs, rows).astype(bf16))
    gr = (gate * picked).astype(bf16)
    gr_out[0] = gr
    turn = gate * jnp.sum(picked * result_ref[0].astype(f32), axis=1, keepdims=True)
    total = None
    for at in range(0, up.shape[1], chunk):
        cols = slice(at, at + chunk)
        gh = (mm(gr, down[cols, :], NT) * slope_ref[0, :, cols].astype(f32)).astype(bf16)
        for r in gh_out:
            r[0, :, cols] = gh
        part = mm(gh, up[:, cols], NT)
        total = part if total is None else total + part
    router_out[0] = jnp.sum(turn * c_ref[0].astype(f32), axis=0, keepdims=True)
    router_row = jnp.sum(mine_ref[...] * router_ref[0].astype(f32), axis=0, keepdims=True)
    back = total + turn * router_row
    put_rows(mm(hot_low, back.astype(bf16), TN), own, sib)


def perceptron_kernel(n, chunk, *refs):
    x_refs, refs = refs[:n], refs[n:]
    mask_ref, slot_ref, router_ref, mine_ref, up, down, *outs = refs
    forward_body(x_refs, mask_ref, slot_ref, router_ref, mine_ref, up, down, chunk, outs)


def perceptron_back_kernel(n, rows, chunk, *refs):
    g_refs, refs = refs[:n], refs[n:]
    slot_ref, router_ref, mine_ref, up, down, c_ref, slope, result, gate, *outs = refs
    if g_refs[0].shape[1] > rows:
        home_out, *outs = outs
        home_out[0] = home_of(g_refs, rows, mine_ref[...])
    kept = (c_ref, slope, result, gate)
    backward_body(g_refs, rows, slot_ref, router_ref, mine_ref, up, down, chunk, kept, outs)


def ff_gradient_kernel(sides, given, *refs):
    side_refs, (up, down, *refs) = refs[:sides], refs[sides:]
    up_out, down_out = refs[given:]
    features = up.shape[0]
    copies, gr = (r[...].reshape(-1, features) for r in side_refs)
    active, slope = gelu_parts(mm(up[...], copies, ((0,), (1,))))
    gh = (mm(down[...], gr, NT) * slope).astype(bf16)
    up_out[...] = mm(gh, copies).T
    down_out[...] = mm(active.astype(bf16), gr)


def ff_gradient(sides, up, down, layer, width, start, steps, before):
    features = up.shape[2]
    given, count = len(before), len(sides)
    shapes = [jax.ShapeDtypeStruct(a.shape, f32) for a in (up, down)]
    specs = [
        pl.BlockSpec((None, None, features, width), lambda j: (layer, 0, 0, start + j)),
        pl.BlockSpec((None, None, width, features), lambda j: (layer, 0, start + j, 0)),
    ]
    return pl.pallas_call(
        partial(ff_gradient_kernel, count, given),
        grid=(steps,),
        in_specs=[whole(a) for a in sides]
        + specs
        + [pl.BlockSpec(memory_space=pl.ANY)] * given,
        out_specs=specs,
        out_shape=shapes,
        input_output_aliases={count + 2 + j: j for j in range(given)},
        compiler_params=pltpu.CompilerParams(
            dimension_semantics=("arbitrary",), vmem_limit_bytes=60 * MIB
        ),
        cost_estimate=pl.CostEstimate(flops=1, bytes_accessed=1, transcendentals=0),
        name="ff_gradient",
    )(*sides, up, down, *before)


def widen_kernel(layers, *refs):
    outs = refs[-2:]
    for j, out in enumerate(outs):
        for layer in range(layers):
            out[layer, 0] = refs[j * layers + layer][...].astype(f32)


def widen(groups):
    layers = len(groups[0])
    ins = [(a, whole, "hbm") for items in groups for a in items]
    outs = [((layers, 1, *items[0].shape), f32, whole) for items in groups]
    return run("widen", partial(widen_kernel, layers), 1, ins, outs, 0, 16)


def assemble_kernel(n, layers, tasks, me_ref, *refs):
    found, (key_out, value_out, column_out, vector_out, late_out) = refs[:n], refs[n:]
    share = key_out.shape[1] // n
    columns, vectors, late = column_out.shape[1], vector_out.shape[0], late_out.shape[0]
    at = layers * 2 * share
    vector_sum = late_sum = 0.0
    for d in range(n):
        place = me_ref[0] ^ d
        held = found[d][...].astype(f32)
        rows = pl.ds(pl.multiple_of(place * share, 8), share)
        for layer in range(layers):
            key_out[layer, rows, :] = held[2 * layer * share : (2 * layer + 1) * share]
            value_out[layer, rows, :] = held[(2 * layer + 1) * share : (2 * layer + 2) * share]
        late_sum = late_sum + held[at : at + late]
        vector_sum = vector_sum + held[at + late : at + late + vectors]
        column_out[place] = held[at + late + vectors : at + late + vectors + columns]
    vector_out[...] = vector_sum
    late_out[...] = late_sum


def flat(ref):
    images, rows, features = ref.shape
    return ref[...].astype(f32).reshape(images * rows, features)


def normed(state):
    centered = state - jnp.mean(state, axis=-1, keepdims=True)
    inverse = lax.rsqrt(jnp.mean(centered * centered, axis=-1, keepdims=True) + epsilon)
    return centered * inverse, inverse


def enter_kernel(state_ref, gain_ref, shift_ref, extra_ref, named_ref, low_out, sent_out):
    unit, _ = normed(flat(state_ref))
    low = (unit * gain_ref[...] + shift_ref[...]).reshape(low_out.shape).astype(bf16)
    low_out[...] = low
    images = low.shape[0]
    for i in range(images):
        sent_out[i] = low[i]
        sent_out[images + i] = extra_ref[i]
    sent_out[2 * images] = named_ref[...]


def join_kernel(parts, last, *refs):
    part_refs, refs = refs[:parts], refs[parts:]
    state_ref, gain_ref, shift_ref, state_out, *low_out = refs
    state = flat(state_ref)
    added = flat(part_refs[0])
    for r in part_refs[1:]:
        added = added + flat(r)
    state = state + added
    state_out[...] = state.reshape(state_out.shape)
    if not last:
        unit, _ = normed(state)
        rows = unit * gain_ref[...] + shift_ref[...]
        low_out[0][...] = rows.reshape(low_out[0].shape).astype(bf16)


def join_back_kernel(parts, *refs):
    part_refs, refs = refs[:parts], refs[parts:]
    grad_ref, before_ref, after_ref, low_ref, router_ref, mask_ref, gain_ref, *refs = refs
    grad_out, low_out, gain_out, shift_out, *more = refs
    images, rows, features = grad_ref.shape
    total = part_refs[0][...].astype(f32)
    for r in part_refs[1:]:
        total = total + r[...].astype(f32)
    if total.ndim == 3:
        (home_out,) = more
        back = total.reshape(images * rows, features)
    else:
        home_out, share_out = more
        step = -(-rows // 16) * 16
        back = jnp.concatenate([total[i * step : i * step + rows] for i in range(images)], axis=0)
        share_out[...] = total[images * step :].astype(bf16)
    grad = flat(grad_ref)
    before = flat(before_ref)
    share = jnp.sum(grad * (flat(after_ref) - before), axis=1, keepdims=True)
    highest = lax.Precision.HIGHEST
    taken, homes = [], []
    for i in range(images):
        router = router_ref[i]
        gates = masked_softmax(mm(low_ref[i], router, NT), mask_ref[i] > 0.5, 1)
        weighted = gates * share[i * rows : (i + 1) * rows]
        taken.append(mm(weighted, router.astype(f32), NN, highest))
        homes.append(-mm(weighted, low_ref[i].astype(f32), TN, highest))
        home_out[i] = homes[-1]
    back = back - jnp.concatenate(taken, axis=0)
    unit, inverse = normed(before)
    gain_out[...] = jnp.sum(back * unit, axis=0, keepdims=True)
    shift_out[...] = jnp.sum(back, axis=0, keepdims=True)
    back = back * gain_ref[...]
    back = back - jnp.mean(back, axis=1, keepdims=True)
    back = back - unit * jnp.mean(back * unit, axis=1, keepdims=True)
    grad = grad + inverse * back
    grad_out[...] = grad.reshape(grad_out.shape)
    for i in range(images):
        sent = jnp.concatenate([grad[i * rows : (i + 1) * rows], homes[i]], axis=0)
        low_out[i] = sent.astype(bf16)


def pair(array, offset):
    size = lax.axis_size("expert")
    return lax.ppermute(array, "expert", [(i, i ^ offset) for i in range(size)])


def gather(array, beside=None):
    size = lax.axis_size("expert")
    found = {0: array}
    for d in range(size - 2, 0, -2):
        found[d] = pair(array, d)
    if beside is not None:
        arrived = [found[d] for d in range(2, size, 2)]
        beside(arrived)
        found.update(zip(range(2, size, 2), arrived))
    for d in range(0, size, 2):
        found[d + 1] = pair(found[d], 1)
    return [found[d] for d in range(size)]


def scatter(own, sib, later=None):
    other = pair(sib, 1)
    sums = [add_low(own[j], other[j]) for j in range(own.shape[0])]
    if later:
        *sums, later[-1] = lax.optimization_barrier((*sums, later[-1]))
    return [v if j == 0 else pair(v, 2 * j) for j, v in enumerate(sums)]


def add_low(left, right):
    return (left.astype(f32) + right.astype(f32)).astype(bf16)


def dp_pair(array, offset):
    size = lax.axis_size("dp")
    return lax.ppermute(array, "dp", [(i, i ^ offset) for i in range(size)])


def dp_add(array, beside):
    size = lax.axis_size("dp")
    if size & (size - 1) or size > 4:
        return lax.psum(array, "dp")
    arrived = [dp_pair(array, d) for d in range(1, size)]
    if arrived:
        beside(arrived)
    terms = [v.astype(f32) for v in (array, *arrived)]
    while len(terms) > 1:
        terms = [left + right for left, right in zip(terms[::2], terms[1::2])]
    return terms[0].astype(bf16)


def local(
    inputs,
    attention_routes,
    perceptron_routes,
    task_index,
    attention_gain,
    attention_shift,
    perceptron_gain,
    perceptron_shift,
    key_weight,
    value_weight,
    query_weight,
    output_weight,
    up_weight,
    down_weight,
    attention_router,
    perceptron_router,
    cotangent,
):
    n = lax.axis_size("expert")
    me = lax.axis_index("expert").astype(jnp.int32)
    me_dp = lax.axis_index("dp").astype(jnp.int32)[None]
    dp = lax.axis_size("dp")
    images, rows, features = inputs.shape
    layers = key_weight.shape[0]
    hidden = up_weight.shape[-1]
    few = dp & (dp - 1) == 0 and dp <= 4 and features % (16 * dp) == 0
    copies_all, gr_all = {}, {}
    top = attention_routes.shape[-1]
    tasks = attention_router.shape[1]
    capacity = min(rows, rows * top // n * 4 // 3)
    slots = n * capacity
    total = n * rows
    chunk = 384
    width = 256
    mine = (jnp.arange(n, dtype=jnp.int32) == me).astype(f32)[:, None]

    routes = jnp.stack([attention_routes, perceptron_routes])
    named = (routes[..., None] == jnp.arange(n, dtype=jnp.int32)).any(axis=-2)
    home_mask = named.astype(f32)
    plane = named.astype(bf16).transpose(3, 0, 1, 2, 4).reshape(rows, -1)
    marks = plane.shape[1]
    plane = jnp.pad(plane, ((0, 0), (0, features - marks)))
    state = inputs.astype(f32)
    low, sent = run(
        "enter",
        enter_kernel,
        1,
        [
            (a, whole, "hbm")
            for a in (inputs, attention_gain[:1], attention_shift[:1], cotangent, plane)
        ],
        [((images, rows, features), bf16, whole), ((2 * images + 1, rows, features), bf16, whole)],
        10**6,
        16,
    )
    x_all = gather(sent)
    cotangent_all = [(a, per_image_after(images), "hbm") for a in x_all]
    all_masks = jnp.stack([a[2 * images, :, :marks] for a in x_all])
    all_masks = all_masks.reshape(n, rows, 2, layers, images, n).transpose(2, 3, 4, 5, 0, 1)
    all_masks = all_masks.reshape(2, layers, images, n, total)
    mine_mask = jnp.einsum(
        "kliet,e->klit", all_masks, mine[:, 0].astype(bf16), preferred_element_type=f32
    )
    blocks = mine_mask.reshape(2, layers, images, n, rows)
    earlier = jnp.tril(jnp.ones((rows, rows), bf16), -1)
    position = jnp.einsum(
        "klibr,qr->klibq", blocks.astype(bf16), earlier, preferred_element_type=f32
    )
    position = position.astype(jnp.int32) + jnp.arange(n, dtype=jnp.int32)[:, None] * capacity
    slot = jnp.where(blocks > 0.5, position, -1).reshape(2, layers, images, 1, total)
    masks = all_masks.astype(f32)
    routers = (
        attention_router[:, task_index].transpose(0, 1, 3, 2),
        perceptron_router[:, task_index].transpose(0, 1, 3, 2),
    )

    row_shape = (images, rows, features)
    part_shape = (n // 2, images, rows, features)
    slot_shape = (images, slots, features)
    all_shape = (images, total, features)
    gate_shape = (images, slots, 1)
    wide_shape = (images, slots, hidden)
    probs_shape = (images, HEADS, total, slots)
    router_shape = (images, 1, features)
    part_rows = features // n
    step = -(-rows // 16) * 16
    back_shape = (n // 2, images * step + 2 * part_rows, features)
    partial_rows = (part_shape, bf16, per_image_second)
    slot_rows = (slot_shape, bf16, per_image, "hbm")
    all_rows = (all_shape, bf16, per_image, "hbm")
    wide_rows = (wide_shape, bf16, per_image, "hbm")
    gate_rows = (gate_shape, f32, per_image, "hbm")
    wide_kept = [] if few else [wide_rows]
    router_rows = (router_shape, f32, per_image, "hbm")
    flop_small = 2 * images * slots * features * features
    flop_core = 2 * images * slots * total * features
    flop_wide = 2 * images * slots * features * hidden

    def image(array):
        return (array, per_image)

    def const(array):
        return (array, whole)

    def held_image(array):
        return (array, per_image, "hbm")

    def held(array):
        return (array, whole, "hbm")

    def route_sets(kind, layer):
        return [
            (masks, at_set(kind, layer), "hbm"),
            (slot, at_set(kind, layer), "hbm"),
            (routers[kind], at_set(layer), "hbm"),
            held(mine),
        ]

    def join(parts, state, gain, shift):
        last = gain is None
        if last:
            gain = shift = jnp.zeros((1, features), f32)
        outs = [(row_shape, f32, whole)] + ([] if last else [(row_shape, bf16, whole)])
        ins = [const(a) for a in (*parts, state)] + [held(a) for a in (gain, shift)]
        return run("join", partial(join_kernel, len(parts), last), 1, ins, outs, 10**6, 16)

    def join_back(parts, grad, before, after, low, kind, layer, gain):
        ins = [const(a) for a in (*parts, grad)]
        ins += [held(a) for a in (before, after, low)]
        ins += [(routers[kind], set_whole(layer), "hbm")]
        ins += [(home_mask, set_whole(kind, layer), "hbm"), held(gain)]
        outs = [
            (row_shape, f32, whole),
            ((images, rows + n, features), bf16, whole),
            ((1, features), f32, whole),
            ((1, features), f32, whole),
            ((images, n, features), f32, whole),
        ]
        if parts[0].ndim == 2:
            outs.append(((2 * part_rows, features), bf16, whole))
        return run("join_back", partial(join_back_kernel, len(parts)), 1, ins, outs, 10**6, 16)

    kept = []
    for l in range(layers):
        weights = [key_weight, value_weight, query_weight, output_weight]
        own, sib, *saved = run(
            "attend",
            partial(attend_kernel, n),
            images,
            [image(a) for a in x_all]
            + route_sets(0, l)
            + [(w, at_layer(l), "hbm") for w in weights],
            [partial_rows, partial_rows, all_rows, slot_rows, slot_rows, all_rows, all_rows]
            + [(probs_shape, bf16, per_image, "hbm"), slot_rows, slot_rows, gate_rows],
            2 * flop_core + 6 * flop_small,
            32,
            [pltpu.VMEM((features, total), bf16), pltpu.VMEM((features, slots), f32)],
        )
        low_a = low
        middle, low = join(
            scatter(own, sib), state, perceptron_gain[l : l + 1], perceptron_shift[l : l + 1]
        )
        x_all = gather(low)
        ff_weights = [up_weight, down_weight]
        route_ins = route_sets(1, l)
        last = l == layers - 1
        if last:
            for j in copies_all:
                x_all[-1], copies_all[j] = lax.optimization_barrier((x_all[-1], copies_all[j]))
        own, sib, copies, slope, result, gate, *active = run(
            "perceptron",
            partial(perceptron_kernel, n, chunk),
            images,
            [image(a) for a in x_all] + route_ins + [(w, at_layer(l), "hbm") for w in ff_weights],
            [partial_rows, partial_rows, slot_rows, wide_rows, slot_rows, gate_rows] + wide_kept,
            2 * flop_wide,
            32,
        )
        kept_ff = (copies, slope, result, gate)
        if few:
            copies_all[l] = lax.all_gather(copies, "dp", axis=0, tiled=False)
        parts = scatter(own, sib)
        if last:
            (after,) = join(parts, middle, None, None)
            low_next = None
        else:
            after, low_next = join(
                parts, middle, attention_gain[l + 1 : l + 2], attention_shift[l + 1 : l + 2]
            )
        kept.append((state, low_a, saved, middle, low, copies, active, kept_ff, after))
        state = after
        low = low_next
        if not last:
            x_all = gather(low)

    grad = cotangent.astype(f32)
    grad_low = None
    gains, columns, shares, ff_parts, qo_parts = [], [], [], [], []
    steps = hidden // width
    halves = ((0, steps // 2), (steps // 2, steps - steps // 2))
    waiting = [(l, *half) for l in range(layers) for half in halves[::-1]] if few else []
    written, experts = [()], []

    def ff_step(arrived, times=2, last=False):
        for l, start, count in [waiting.pop() for _ in range(times) if waiting]:
            written[0] = ff_gradient(
                [copies_all[l], gr_all[l]],
                up_weight,
                down_weight,
                l,
                width,
                start,
                count,
                written[0],
            )
        if few:
            due = experts if last else []
            arrived[-1], written[0], experts[: len(due)] = lax.optimization_barrier(
                (arrived[-1], written[0], due)
            )
    for l in range(layers - 1, -1, -1):
        state, low_a, saved, middle, low_m, copies, active, kept_ff, after = kept[l]
        ff_weights = [up_weight, down_weight]
        last = l == layers - 1
        g_all = cotangent_all if last else [image(a) for a in gather(grad_low)]
        outs = run(
            "perceptron_back",
            partial(perceptron_back_kernel, n, rows, chunk),
            images,
            g_all
            + route_sets(1, l)[1:]
            + [(w, at_layer(l), "hbm") for w in ff_weights]
            + [(a, per_image, "hbm") for a in kept_ff],
            [router_rows] * (not last)
            + [partial_rows, partial_rows, slot_rows, router_rows]
            + wide_kept,
            2 * flop_wide,
            32,
        )
        if not last:
            columns[-1] = columns[-1] + outs[0]
            outs = outs[1:]
        own, sib, gr, router_m, *gh = outs
        parts = scatter(own, sib)
        if few:
            gr_all[l] = lax.all_gather(gr, "dp", axis=0, tiled=False)
            if not last:
                parts[-1], copies_all[l + 1], gr_all[l + 1] = lax.optimization_barrier(
                    (parts[-1], copies_all[l + 1], gr_all[l + 1])
                )
        else:
            up_part = jnp.einsum("isd,isf->df", copies, gh[0], preferred_element_type=f32)
            down_part = jnp.einsum("isf,isd->fd", active[0], gr, preferred_element_type=f32)
            both = (up_part.astype(bf16), down_part.astype(bf16))
            ff_parts.append(lax.psum(both, "dp"))
        grad, grad_low, gain_m, shift_m, _ = join_back(
            parts,
            grad,
            middle,
            after,
            low_m,
            1,
            l,
            perceptron_gain[l : l + 1],
        )
        columns.append(router_m)
        g_all = gather(grad_low)
        x, copies, queries, keys, values, probs, mixed, result, gate = saved
        weights = [key_weight, value_weight, query_weight, output_weight]
        own, sib, gr_a, dq, router_a, home = run(
            "attend_back",
            partial(attend_back_kernel, n, rows),
            images,
            [image(a) for a in g_all]
            + [(me[None], in_smem)]
            + route_sets(0, l)[1:]
            + [(w, at_layer(l), "hbm") for w in weights]
            + [(a, per_image, "hbm") for a in saved],
            [(back_shape, bf16, whole), (back_shape, bf16, whole)]
            + [slot_rows, slot_rows, router_rows, router_rows],
            4 * flop_core + 14 * flop_small,
            32,
            [pltpu.VMEM((features, features), f32)] * 2
            + [
                pltpu.VMEM((slots, features), bf16),
                pltpu.VMEM((features, total), bf16),
                pltpu.VMEM((features, slots), f32),
                pltpu.VMEM((total, features), bf16),
                pltpu.VMEM((total, features), bf16),
            ],
        )
        columns[-1] = columns[-1] + home
        columns.append(router_a)
        later = [gr_all[layers - 1]] if few and l == 0 < layers - 1 else []
        parts = scatter(own, sib, later)
        if later:
            gr_all[layers - 1] = later[0]
        both = (
            jnp.einsum("isd,isf->df", copies, dq, preferred_element_type=f32).astype(bf16),
            jnp.einsum("isf,isd->fd", mixed, gr_a, preferred_element_type=f32).astype(bf16),
        )
        parts[-1], *both = lax.optimization_barrier((parts[-1], *both))
        qo_parts.append(both)
        if few and l < layers - 1:
            parts[-1], gr_all[l] = lax.optimization_barrier((parts[-1], gr_all[l]))
            if l == 0:
                ff_step(parts, 1)
        grad, grad_low, gain_a, shift_a, late, share = join_back(
            parts,
            grad,
            state,
            middle,
            low_a,
            0,
            l,
            attention_gain[l : l + 1],
        )
        gains.append((gain_a, shift_a, gain_m, shift_m))
        shares.append(share)

    if few:
        qo_parts, gr_all[0] = lax.optimization_barrier((qo_parts, gr_all[0]))

    experts += list(zip(*lax.psum(qo_parts, "dp")))
    picked = (task_index[:, None] == jnp.arange(tasks, dtype=jnp.int32)[None, :]).astype(f32)
    highest = lax.Precision.HIGHEST
    columns = jnp.stack([c[:, 0] for c in columns[::-1]])
    columns = jnp.einsum("it,lid->ltd", picked, columns, precision=highest)
    late = jnp.einsum("it,ied->ted", picked, late, precision=highest)
    vectors = [v for items in gains[::-1] for v in items]
    payload = [
        *shares[::-1],
        late.reshape(tasks * n, features).astype(bf16),
        *[v.astype(bf16) for v in vectors],
        columns.reshape(layers * 2 * tasks, features).astype(bf16),
    ]
    used = sum(p.shape[0] for p in payload)
    payload.append(jnp.zeros((-used % 16, features), bf16))
    shared = dp_add(jnp.concatenate(payload, axis=0), ff_step)

    def end(arrived):
        ff_step(arrived, len(waiting), True)

    found = gather(shared, end)
    if few:
        experts = [*widen([items[::-1] for items in experts]), *written[0]]
    else:
        experts = [jnp.stack(items[::-1]).astype(f32)[:, None] for items in experts]
        experts += [jnp.stack(items[::-1]).astype(f32)[:, None] for items in zip(*ff_parts)]
    matrix = ((layers, features, features), f32, whole)
    keys, values, columns, vectors, late = run(
        "assemble",
        partial(assemble_kernel, n, layers, tasks),
        1,
        [(me[None], in_smem)] + [const(a) for a in found],
        [
            matrix,
            matrix,
            ((n, layers * 2 * tasks, features), f32, whole),
            ((len(vectors), features), f32, whole),
            ((tasks * n, features), f32, whole),
        ],
        0,
        24,
    )
    columns = columns.reshape(n, layers, 2, tasks, features).transpose(2, 1, 3, 4, 0)
    late = late.reshape(tasks, n, features).transpose(0, 2, 1)
    attention_columns = jnp.concatenate([columns[0, :1] + late, columns[0, 1:]], axis=0)
    vectors = vectors.reshape(layers, 4, features).transpose(1, 0, 2)
    return (
        kept[-1][-1],
        grad,
        *(vectors[j] for j in range(4)),
        keys,
        values,
        *experts,
        attention_columns,
        columns[1],
    )


def solution(mesh):
    in_specs = (
        P("dp", "expert", None),
        P(None, "dp", "expert", None),
        P(None, "dp", "expert", None),
        P("dp"),
        P(),
        P(),
        P(),
        P(),
        P(),
        P(),
        P(None, "expert", None, None),
        P(None, "expert", None, None),
        P(None, "expert", None, None),
        P(None, "expert", None, None),
        P(),
        P(),
        P("dp", "expert", None),
    )
    out_specs = (
        P("dp", "expert", None),
        P("dp", "expert", None),
        P(),
        P(),
        P(),
        P(),
        P(),
        P(),
        P(None, "expert", None, None),
        P(None, "expert", None, None),
        P(None, "expert", None, None),
        P(None, "expert", None, None),
        P(),
        P(),
    )
    return jax.shard_map(local, mesh=mesh, in_specs=in_specs, out_specs=out_specs, check_vma=False)
```

```python
from functools import partial

import jax
import jax.numpy as jnp
from jax import lax
from jax.experimental import pallas as pl
from jax.experimental.pallas import tpu as pltpu
from jax.sharding import PartitionSpec as P

HEADS = 6
epsilon = 1e-06
f32, bf16 = jnp.float32, jnp.bfloat16
NN, NT, TN = ((1,), (0,)), ((1,), (1,)), ((0,), (0,))
MIB = 1 << 20


def mm(left, right, dims=NN, precision=None):
    return lax.dot_general(
        left, right, (dims, ((), ())), preferred_element_type=f32, precision=precision
    )


def whole(array):
    rank = len(array.shape)
    return pl.BlockSpec(array.shape, lambda i: (0,) * rank)


def per_image(array):
    rank = len(array.shape)
    return pl.BlockSpec((1,) + tuple(array.shape[1:]), lambda i: (i,) + (0,) * (rank - 1))


def per_image_after(first):
    def maker(array):
        rank = len(array.shape)
        return pl.BlockSpec(
            (1,) + tuple(array.shape[1:]), lambda i: (first + i,) + (0,) * (rank - 1)
        )

    return maker


def per_image_second(array):
    rank = len(array.shape)
    return pl.BlockSpec(
        (array.shape[0], 1) + tuple(array.shape[2:]), lambda i: (0, i) + (0,) * (rank - 2)
    )


def at_set(*lead):
    def maker(array):
        rank = len(array.shape)
        count = len(lead)
        return pl.BlockSpec(
            (None,) * count + (1,) + tuple(array.shape[count + 1 :]),
            lambda i: (*lead, i) + (0,) * (rank - count - 1),
        )

    return maker


def set_whole(*lead):
    def maker(array):
        rank, count = len(array.shape), len(lead)
        return pl.BlockSpec(
            (None,) * count + tuple(array.shape[count:]),
            lambda i: (*lead,) + (0,) * (rank - count),
        )

    return maker


def at_layer(layer):
    def maker(array):
        rank = len(array.shape)
        lead = rank - 2
        return pl.BlockSpec(
            (None,) * lead + tuple(array.shape[lead:]),
            lambda i: (layer,) + (0,) * (rank - 1),
        )

    return maker


def in_smem(array):
    return pl.BlockSpec(memory_space=pltpu.SMEM)


def run(name, kernel, images, ins, outs, flops, limit, scratch=()):
    ins = [
        (pltpu.with_memory_space_constraint(a, pltpu.HBM) if pinned else a, maker)
        for a, maker, *pinned in ins
    ]
    shapes = [jax.ShapeDtypeStruct(shape, dtype) for shape, dtype, *_ in outs]
    moved = sum(a.size * a.dtype.itemsize for a, _ in ins)
    moved += sum(s.size * s.dtype.itemsize for s in shapes)
    out_specs = [item[2](s) for s, item in zip(shapes, outs)]
    shapes = [pltpu.HBM(*item[:2]) if len(item) > 3 else s for s, item in zip(shapes, outs)]
    return pl.pallas_call(
        kernel,
        grid=(images,),
        in_specs=[maker(a) for a, maker in ins],
        out_specs=out_specs,
        out_shape=shapes,
        scratch_shapes=list(scratch),
        compiler_params=pltpu.CompilerParams(
            dimension_semantics=("arbitrary",), vmem_limit_bytes=limit * MIB
        ),
        cost_estimate=pl.CostEstimate(flops=1, bytes_accessed=1, transcendentals=0),
        name=name,
    )(*[a for a, _ in ins])


def rows_of(refs, rows=None):
    return jnp.concatenate([r[0].astype(f32)[:rows] for r in refs], axis=0)


def home_of(refs, rows, mine):
    total = refs[0][0].astype(f32)[rows:]
    for r in refs[1:]:
        total = total + r[0].astype(f32)[rows:]
    return jnp.sum(total * mine, axis=0, keepdims=True)


def put_rows(rows, own_ref, sib_ref):
    half = own_ref.shape[0]
    size = own_ref.shape[2]
    for d in range(2 * half):
        target = own_ref if d % 2 == 0 else sib_ref
        target[d // 2, 0] = rows[d * size : (d + 1) * size].astype(bf16)


def one_hot(slot_ref, slots):
    slot = slot_ref[0]
    spots = lax.broadcasted_iota(jnp.int32, (slots, slot.shape[1]), 0)
    return spots == slot


def masked_softmax(logits, mask, axis):
    top = jnp.max(jnp.where(mask, logits, -3e38), axis=axis, keepdims=True)
    weights = jnp.where(mask, jnp.exp(jnp.minimum(logits - top, 0.0)), 0.0)
    return weights / jnp.sum(weights, axis=axis, keepdims=True)


def own_gate(rows_low, router, mask8, mine):
    gates = masked_softmax(mm(router, rows_low, NT), mask8 > 0.5, 0)
    return jnp.sum(gates * mine, axis=0, keepdims=True)


def attend_kernel(n, *refs):
    x_refs, refs = refs[:n], refs[n:]
    mask_ref, slot_ref, router_ref, mine_ref, wk, wv, wq, wo, *refs = refs
    own, sib, x_out, c_out, q_out, k_out, v_out, p_out, mixed_out, *refs = refs
    result_out, gate_out, values_t, mixed_t = refs
    slots, features = c_out.shape[1:]
    size = features // HEADS
    x = rows_of(x_refs).astype(bf16)
    x_out[0] = x
    hot = one_hot(slot_ref, slots)
    hot_low = hot.astype(f32).astype(bf16)
    gate_row = own_gate(x, router_ref[0], mask_ref[0].astype(f32), mine_ref[...])
    gate = jnp.sum(jnp.where(hot, gate_row, 0.0), axis=1, keepdims=True)
    gate_out[0] = gate
    copies = mm(hot_low, x).astype(bf16)
    c_out[0] = copies
    queries = (mm(copies, wq[...]).astype(bf16).astype(f32) * size ** (-0.5)).astype(bf16)
    q_out[0] = queries
    keys = mm(x, wk[...]).astype(bf16)
    k_out[0] = keys
    values = mm(x, wv[...])
    v_out[0] = values.astype(bf16)
    values_t[...] = values.T.astype(bf16)
    low = lax.broadcasted_iota(jnp.int32, (slots, 2 * size), 1) < size
    zero = jnp.zeros((slots, 2 * size), bf16)

    def two_heads(pair_index, carry):
        start = pl.multiple_of(pair_index * 2 * size, 2 * size)
        lanes = pl.ds(start, 2 * size)
        for half in range(2):
            keep = low if half == 0 else jnp.logical_not(low)
            scores = mm(k_out[0, :, lanes], jnp.where(keep, q_out[0, :, lanes], zero), NT)
            weights = jnp.exp(scores - jnp.max(scores, axis=0, keepdims=True))
            inverse = 1.0 / jnp.sum(weights, axis=0, keepdims=True)
            probs = (weights * inverse).astype(bf16)
            p_out[0, 2 * pair_index + half] = probs
            rows = pl.ds(pl.multiple_of(start + half * size, size), size)
            mixed_t[rows, :] = mm(values_t[rows, :], probs)
        return carry

    lax.fori_loop(0, HEADS // 2, two_heads, 0, unroll=True)
    mixed = mixed_t[...].T.astype(bf16)
    mixed_out[0] = mixed
    result = mm(mixed, wo[...]).astype(bf16)
    result_out[0] = result
    put_rows(mm(hot_low, (gate * result.astype(f32)).astype(bf16), TN), own, sib)


def attend_back_kernel(n, rows, *refs):
    g_refs, refs = refs[:n], refs[n:]
    me_ref, slot_ref, router_ref, mine_ref, wk, wv, wq, wo, *refs = refs
    x_ref, c_ref, q_ref, k_ref, v_ref, p_ref, mixed_ref, result_ref, gate_ref, *refs = refs
    own, sib, gr_out, dq_out, router_out, home_out, key_sum, value_sum, *refs = refs
    grad_mixed, keys_t, dq_t, dk_wide, dv_wide = refs
    image = pl.program_id(0)
    slots, features = c_ref.shape[1:]
    size = features // HEADS
    hot = one_hot(slot_ref, slots)
    hot_low = hot.astype(f32).astype(bf16)
    gate = gate_ref[0]
    picked = mm(hot_low, rows_of(g_refs, rows).astype(bf16))
    home_out[0] = home_of(g_refs, rows, mine_ref[...])
    gr = (gate * picked).astype(bf16)
    gr_out[0] = gr
    turn = gate * jnp.sum(picked * result_ref[0].astype(f32), axis=1, keepdims=True)
    grad_mixed[...] = mm(gr, wo[...], NT).astype(bf16)
    keys_t[...] = k_ref[0].astype(f32).T.astype(bf16)
    low = lax.broadcasted_iota(jnp.int32, (slots, 2 * size), 1) < size
    zero = jnp.zeros((slots, 2 * size), bf16)

    def two_heads(pair_index, carry):
        start = pl.multiple_of(pair_index * 2 * size, 2 * size)
        lanes = pl.ds(start, 2 * size)
        dk_part = dv_part = 0.0
        for half in range(2):
            keep = low if half == 0 else jnp.logical_not(low)
            q_head = jnp.where(keep, q_ref[0, :, lanes], zero)
            gm_head = jnp.where(keep, grad_mixed[:, lanes], zero)
            probs = p_ref[0, 2 * pair_index + half]
            dv_part = dv_part + mm(probs, gm_head)
            probs_wide = probs.astype(f32)
            grad_probs = mm(v_ref[0, :, lanes], gm_head, NT)
            inner = jnp.sum(probs_wide * grad_probs, axis=0, keepdims=True)
            grad_scores = (probs_wide * (grad_probs - inner)).astype(bf16)
            rows = pl.ds(pl.multiple_of(start + half * size, size), size)
            dq_t[rows, :] = mm(keys_t[rows, :], grad_scores)
            dk_part = dk_part + mm(grad_scores, q_head)
        dk_wide[:, lanes] = dk_part.astype(bf16)
        dv_wide[:, lanes] = dv_part.astype(bf16)
        return carry

    lax.fori_loop(0, HEADS // 2, two_heads, 0)
    dq = (dq_t[...].T * size ** (-0.5)).astype(bf16)
    dq_out[0] = dq
    dk, dv = dk_wide[...], dv_wide[...]
    copies = c_ref[0].astype(f32)
    router_out[0] = jnp.sum(turn * copies, axis=0, keepdims=True)
    router_row = jnp.sum(mine_ref[...] * router_ref[0].astype(f32), axis=0, keepdims=True)
    back = mm(dq, wq[...], NT) + turn * router_row
    back = mm(hot_low, back.astype(bf16), TN) + mm(dk, wk[...], NT) + mm(dv, wv[...], NT)
    step = -(-rows // 16) * 16
    at = pl.ds(pl.multiple_of(image * step, 16), step)
    gap = jnp.zeros((step - rows, features), f32)
    for d in range(n):
        target = own if d % 2 == 0 else sib
        part = back[d * rows : (d + 1) * rows]
        if step > rows:
            part = jnp.concatenate([part, gap], axis=0)
        target[d // 2, at, :] = part.astype(bf16)
    key_part, value_part = mm(x_ref[0], dk, TN), mm(x_ref[0], dv, TN)

    @pl.when(image == 0)
    def _():
        key_sum[...] = key_part
        value_sum[...] = value_part

    @pl.when(image > 0)
    def _():
        key_sum[...] += key_part
        value_sum[...] += value_part

    @pl.when(image == pl.num_programs(0) - 1)
    def _():
        share = features // n
        start = own.shape[1] - 2 * share
        for d in range(n):
            target = own if d % 2 == 0 else sib
            taken = pl.ds(pl.multiple_of((me_ref[0] ^ d) * share, 8), share)
            both = jnp.concatenate([key_sum[taken, :], value_sum[taken, :]], axis=0)
            target[d // 2, start:, :] = both.astype(bf16)


def gelu_parts(hidden):
    phi = 0.5 + 0.5 * lax.erf(hidden * (0.5**0.5))
    bell = jnp.exp(-0.5 * hidden * hidden) * 0.3989422804014327
    return hidden * phi, phi + hidden * bell


def forward_body(x_refs, mask_ref, slot_ref, router_ref, mine_ref, up, down, chunk, outs):
    own, sib, c_out, slope_out, result_out, gate_out, *active_out = outs
    slots = c_out.shape[1]
    x = rows_of(x_refs).astype(bf16)
    hot = one_hot(slot_ref, slots)
    hot_low = hot.astype(f32).astype(bf16)
    gate_row = own_gate(x, router_ref[0], mask_ref[0].astype(f32), mine_ref[...])
    gate = jnp.sum(jnp.where(hot, gate_row, 0.0), axis=1, keepdims=True)
    gate_out[0] = gate
    copies = mm(hot_low, x).astype(bf16)
    c_out[0] = copies
    total = None
    for at in range(0, up.shape[1], chunk):
        cols = slice(at, at + chunk)
        active, slope = gelu_parts(mm(copies, up[:, cols]))
        active = active.astype(bf16)
        for r in active_out:
            r[0, :, cols] = active
        slope_out[0, :, cols] = slope.astype(bf16)
        part = mm(active, down[cols, :])
        total = part if total is None else total + part
    result = total.astype(bf16)
    result_out[0] = result
    put_rows(mm(hot_low, (gate * result.astype(f32)).astype(bf16), TN), own, sib)


def backward_body(g_refs, rows, slot_ref, router_ref, mine_ref, up, down, chunk, kept, outs):
    c_ref, slope_ref, result_ref, gate_ref = kept
    own, sib, gr_out, router_out, *gh_out = outs
    slots = c_ref.shape[1]
    hot_low = one_hot(slot_ref, slots).astype(f32).astype(bf16)
    gate = gate_ref[0]
    picked = mm(hot_low, rows_of(g_refs, rows).astype(bf16))
    gr = (gate * picked).astype(bf16)
    gr_out[0] = gr
    turn = gate * jnp.sum(picked * result_ref[0].astype(f32), axis=1, keepdims=True)
    total = None
    for at in range(0, up.shape[1], chunk):
        cols = slice(at, at + chunk)
        gh = (mm(gr, down[cols, :], NT) * slope_ref[0, :, cols].astype(f32)).astype(bf16)
        for r in gh_out:
            r[0, :, cols] = gh
        part = mm(gh, up[:, cols], NT)
        total = part if total is None else total + part
    router_out[0] = jnp.sum(turn * c_ref[0].astype(f32), axis=0, keepdims=True)
    router_row = jnp.sum(mine_ref[...] * router_ref[0].astype(f32), axis=0, keepdims=True)
    back = total + turn * router_row
    put_rows(mm(hot_low, back.astype(bf16), TN), own, sib)


def perceptron_kernel(n, chunk, *refs):
    x_refs, refs = refs[:n], refs[n:]
    mask_ref, slot_ref, router_ref, mine_ref, up, down, *outs = refs
    forward_body(x_refs, mask_ref, slot_ref, router_ref, mine_ref, up, down, chunk, outs)


def perceptron_back_kernel(n, rows, chunk, *refs):
    g_refs, refs = refs[:n], refs[n:]
    slot_ref, router_ref, mine_ref, up, down, c_ref, slope, result, gate, *outs = refs
    if g_refs[0].shape[1] > rows:
        home_out, *outs = outs
        home_out[0] = home_of(g_refs, rows, mine_ref[...])
    kept = (c_ref, slope, result, gate)
    backward_body(g_refs, rows, slot_ref, router_ref, mine_ref, up, down, chunk, kept, outs)


def ff_gradient_kernel(sides, given, *refs):
    side_refs, (up, down, *refs) = refs[:sides], refs[sides:]
    up_out, down_out = refs[given:]
    features = up.shape[0]
    copies, gr = (r[...].reshape(-1, features) for r in side_refs)
    active, slope = gelu_parts(mm(up[...], copies, ((0,), (1,))))
    gh = (mm(down[...], gr, NT) * slope).astype(bf16)
    up_out[...] = mm(gh, copies).T
    down_out[...] = mm(active.astype(bf16), gr)


def ff_gradient(sides, up, down, layer, width, start, steps, before):
    features = up.shape[2]
    given, count = len(before), len(sides)
    shapes = [jax.ShapeDtypeStruct(a.shape, f32) for a in (up, down)]
    specs = [
        pl.BlockSpec((None, None, features, width), lambda j: (layer, 0, 0, start + j)),
        pl.BlockSpec((None, None, width, features), lambda j: (layer, 0, start + j, 0)),
    ]
    return pl.pallas_call(
        partial(ff_gradient_kernel, count, given),
        grid=(steps,),
        in_specs=[whole(a) for a in sides]
        + specs
        + [pl.BlockSpec(memory_space=pl.ANY)] * given,
        out_specs=specs,
        out_shape=shapes,
        input_output_aliases={count + 2 + j: j for j in range(given)},
        compiler_params=pltpu.CompilerParams(
            dimension_semantics=("arbitrary",), vmem_limit_bytes=60 * MIB
        ),
        cost_estimate=pl.CostEstimate(flops=1, bytes_accessed=1, transcendentals=0),
        name="ff_gradient",
    )(*sides, up, down, *before)


def widen_kernel(layers, *refs):
    outs = refs[-2:]
    for j, out in enumerate(outs):
        for layer in range(layers):
            out[layer, 0] = refs[j * layers + layer][...].astype(f32)


def widen(groups):
    layers = len(groups[0])
    ins = [(a, whole, "hbm") for items in groups for a in items]
    outs = [((layers, 1, *items[0].shape), f32, whole) for items in groups]
    return run("widen", partial(widen_kernel, layers), 1, ins, outs, 0, 16)


def assemble_kernel(n, layers, tasks, me_ref, *refs):
    found, (key_out, value_out, column_out, vector_out, late_out) = refs[:n], refs[n:]
    share = key_out.shape[1] // n
    columns, vectors, late = column_out.shape[1], vector_out.shape[0], late_out.shape[0]
    at = layers * 2 * share
    vector_sum = late_sum = 0.0
    for d in range(n):
        place = me_ref[0] ^ d
        held = found[d][...].astype(f32)
        rows = pl.ds(pl.multiple_of(place * share, 8), share)
        for layer in range(layers):
            key_out[layer, rows, :] = held[2 * layer * share : (2 * layer + 1) * share]
            value_out[layer, rows, :] = held[(2 * layer + 1) * share : (2 * layer + 2) * share]
        late_sum = late_sum + held[at : at + late]
        vector_sum = vector_sum + held[at + late : at + late + vectors]
        column_out[place] = held[at + late + vectors : at + late + vectors + columns]
    vector_out[...] = vector_sum
    late_out[...] = late_sum


def flat(ref):
    images, rows, features = ref.shape
    return ref[...].astype(f32).reshape(images * rows, features)


def normed(state):
    centered = state - jnp.mean(state, axis=-1, keepdims=True)
    inverse = lax.rsqrt(jnp.mean(centered * centered, axis=-1, keepdims=True) + epsilon)
    return centered * inverse, inverse


def enter_kernel(state_ref, gain_ref, shift_ref, extra_ref, named_ref, low_out, sent_out):
    unit, _ = normed(flat(state_ref))
    low = (unit * gain_ref[...] + shift_ref[...]).reshape(low_out.shape).astype(bf16)
    low_out[...] = low
    images = low.shape[0]
    for i in range(images):
        sent_out[i] = low[i]
        sent_out[images + i] = extra_ref[i]
    sent_out[2 * images] = named_ref[...]


def join_kernel(parts, last, *refs):
    part_refs, refs = refs[:parts], refs[parts:]
    state_ref, gain_ref, shift_ref, state_out, *low_out = refs
    state = flat(state_ref)
    added = flat(part_refs[0])
    for r in part_refs[1:]:
        added = added + flat(r)
    state = state + added
    state_out[...] = state.reshape(state_out.shape)
    if not last:
        unit, _ = normed(state)
        rows = unit * gain_ref[...] + shift_ref[...]
        low_out[0][...] = rows.reshape(low_out[0].shape).astype(bf16)


def join_back_kernel(parts, *refs):
    part_refs, refs = refs[:parts], refs[parts:]
    grad_ref, before_ref, after_ref, low_ref, router_ref, mask_ref, gain_ref, *refs = refs
    grad_out, low_out, gain_out, shift_out, *more = refs
    images, rows, features = grad_ref.shape
    total = part_refs[0][...].astype(f32)
    for r in part_refs[1:]:
        total = total + r[...].astype(f32)
    if total.ndim == 3:
        (home_out,) = more
        back = total.reshape(images * rows, features)
    else:
        home_out, share_out = more
        step = -(-rows // 16) * 16
        back = jnp.concatenate([total[i * step : i * step + rows] for i in range(images)], axis=0)
        share_out[...] = total[images * step :].astype(bf16)
    grad = flat(grad_ref)
    before = flat(before_ref)
    share = jnp.sum(grad * (flat(after_ref) - before), axis=1, keepdims=True)
    highest = lax.Precision.HIGHEST
    taken, homes = [], []
    for i in range(images):
        router = router_ref[i]
        gates = masked_softmax(mm(low_ref[i], router, NT), mask_ref[i] > 0.5, 1)
        weighted = gates * share[i * rows : (i + 1) * rows]
        taken.append(mm(weighted, router.astype(f32), NN, highest))
        homes.append(-mm(weighted, low_ref[i].astype(f32), TN, highest))
        home_out[i] = homes[-1]
    back = back - jnp.concatenate(taken, axis=0)
    unit, inverse = normed(before)
    gain_out[...] = jnp.sum(back * unit, axis=0, keepdims=True)
    shift_out[...] = jnp.sum(back, axis=0, keepdims=True)
    back = back * gain_ref[...]
    back = back - jnp.mean(back, axis=1, keepdims=True)
    back = back - unit * jnp.mean(back * unit, axis=1, keepdims=True)
    grad = grad + inverse * back
    grad_out[...] = grad.reshape(grad_out.shape)
    for i in range(images):
        sent = jnp.concatenate([grad[i * rows : (i + 1) * rows], homes[i]], axis=0)
        low_out[i] = sent.astype(bf16)


def pair(array, offset):
    size = lax.axis_size("expert")
    return lax.ppermute(array, "expert", [(i, i ^ offset) for i in range(size)])


def gather(array, beside=None):
    size = lax.axis_size("expert")
    found = {0: array}
    for d in range(size - 2, 0, -2):
        found[d] = pair(array, d)
    if beside is not None:
        arrived = [found[d] for d in range(2, size, 2)]
        beside(arrived)
        found.update(zip(range(2, size, 2), arrived))
    for d in range(0, size, 2):
        found[d + 1] = pair(found[d], 1)
    return [found[d] for d in range(size)]


def scatter(own, sib, later=None):
    other = pair(sib, 1)
    sums = [add_low(own[j], other[j]) for j in range(own.shape[0])]
    if later:
        *sums, later[-1] = lax.optimization_barrier((*sums, later[-1]))
    return [v if j == 0 else pair(v, 2 * j) for j, v in enumerate(sums)]


def add_low(left, right):
    return (left.astype(f32) + right.astype(f32)).astype(bf16)


def dp_pair(array, offset):
    size = lax.axis_size("dp")
    return lax.ppermute(array, "dp", [(i, i ^ offset) for i in range(size)])


def dp_add(array, beside):
    size = lax.axis_size("dp")
    if size & (size - 1) or size > 4:
        return lax.psum(array, "dp")
    arrived = [dp_pair(array, d) for d in range(1, size)]
    if arrived:
        beside(arrived)
    terms = [v.astype(f32) for v in (array, *arrived)]
    while len(terms) > 1:
        terms = [left + right for left, right in zip(terms[::2], terms[1::2])]
    return terms[0].astype(bf16)


def local(
    inputs,
    attention_routes,
    perceptron_routes,
    task_index,
    attention_gain,
    attention_shift,
    perceptron_gain,
    perceptron_shift,
    key_weight,
    value_weight,
    query_weight,
    output_weight,
    up_weight,
    down_weight,
    attention_router,
    perceptron_router,
    cotangent,
):
    n = lax.axis_size("expert")
    me = lax.axis_index("expert").astype(jnp.int32)
    me_dp = lax.axis_index("dp").astype(jnp.int32)[None]
    dp = lax.axis_size("dp")
    images, rows, features = inputs.shape
    layers = key_weight.shape[0]
    hidden = up_weight.shape[-1]
    few = dp & (dp - 1) == 0 and dp <= 4 and features % (16 * dp) == 0
    copies_all, gr_all = {}, {}
    top = attention_routes.shape[-1]
    tasks = attention_router.shape[1]
    capacity = min(rows, rows * top // n * 4 // 3)
    slots = n * capacity
    total = n * rows
    chunk = 768
    width = 256
    mine = (jnp.arange(n, dtype=jnp.int32) == me).astype(f32)[:, None]

    routes = jnp.stack([attention_routes, perceptron_routes])
    named = (routes[..., None] == jnp.arange(n, dtype=jnp.int32)).any(axis=-2)
    home_mask = named.astype(f32)
    plane = named.astype(bf16).transpose(3, 0, 1, 2, 4).reshape(rows, -1)
    marks = plane.shape[1]
    plane = jnp.pad(plane, ((0, 0), (0, features - marks)))
    state = inputs.astype(f32)
    low, sent = run(
        "enter",
        enter_kernel,
        1,
        [
            (a, whole, "hbm")
            for a in (inputs, attention_gain[:1], attention_shift[:1], cotangent, plane)
        ],
        [((images, rows, features), bf16, whole), ((2 * images + 1, rows, features), bf16, whole)],
        10**6,
        16,
    )
    x_all = gather(sent)
    cotangent_all = [(a, per_image_after(images), "hbm") for a in x_all]
    all_masks = jnp.stack([a[2 * images, :, :marks] for a in x_all])
    all_masks = all_masks.reshape(n, rows, 2, layers, images, n).transpose(2, 3, 4, 5, 0, 1)
    all_masks = all_masks.reshape(2, layers, images, n, total)
    mine_mask = jnp.einsum(
        "kliet,e->klit", all_masks, mine[:, 0].astype(bf16), preferred_element_type=f32
    )
    place = jnp.arange(total, dtype=jnp.int32)
    block = place // rows
    earlier = (block[:, None] == block) & (place[:, None] < place)
    position = jnp.einsum(
        "klit,tq->kliq",
        mine_mask.astype(bf16),
        earlier.astype(bf16),
        preferred_element_type=f32,
    )
    slot = position.astype(jnp.int32) + block * capacity
    slot = jnp.where(mine_mask > 0.5, slot, -1)[..., None, :]
    masks = all_masks
    routers = (
        attention_router[:, task_index].transpose(0, 1, 3, 2),
        perceptron_router[:, task_index].transpose(0, 1, 3, 2),
    )

    row_shape = (images, rows, features)
    part_shape = (n // 2, images, rows, features)
    slot_shape = (images, slots, features)
    all_shape = (images, total, features)
    gate_shape = (images, slots, 1)
    wide_shape = (images, slots, hidden)
    probs_shape = (images, HEADS, total, slots)
    router_shape = (images, 1, features)
    part_rows = features // n
    step = -(-rows // 16) * 16
    back_shape = (n // 2, images * step + 2 * part_rows, features)
    partial_rows = (part_shape, bf16, per_image_second)
    slot_rows = (slot_shape, bf16, per_image, "hbm")
    all_rows = (all_shape, bf16, per_image, "hbm")
    wide_rows = (wide_shape, bf16, per_image, "hbm")
    gate_rows = (gate_shape, f32, per_image, "hbm")
    wide_kept = [] if few else [wide_rows]
    router_rows = (router_shape, f32, per_image, "hbm")
    flop_small = 2 * images * slots * features * features
    flop_core = 2 * images * slots * total * features
    flop_wide = 2 * images * slots * features * hidden

    def image(array):
        return (array, per_image)

    def const(array):
        return (array, whole)

    def held_image(array):
        return (array, per_image, "hbm")

    def held(array):
        return (array, whole, "hbm")

    def route_sets(kind, layer):
        return [
            (masks, at_set(kind, layer), "hbm"),
            (slot, at_set(kind, layer), "hbm"),
            (routers[kind], at_set(layer), "hbm"),
            held(mine),
        ]

    def join(parts, state, gain, shift):
        last = gain is None
        if last:
            gain = shift = jnp.zeros((1, features), f32)
        outs = [(row_shape, f32, whole)] + ([] if last else [(row_shape, bf16, whole)])
        ins = [const(a) for a in (*parts, state)] + [held(a) for a in (gain, shift)]
        return run("join", partial(join_kernel, len(parts), last), 1, ins, outs, 10**6, 16)

    def join_back(parts, grad, before, after, low, kind, layer, gain):
        ins = [const(a) for a in (*parts, grad)]
        ins += [held(a) for a in (before, after, low)]
        ins += [(routers[kind], set_whole(layer), "hbm")]
        ins += [(home_mask, set_whole(kind, layer), "hbm"), held(gain)]
        outs = [
            (row_shape, f32, whole),
            ((images, rows + n, features), bf16, whole),
            ((1, features), f32, whole),
            ((1, features), f32, whole),
            ((images, n, features), f32, whole),
        ]
        if parts[0].ndim == 2:
            outs.append(((2 * part_rows, features), bf16, whole))
        return run("join_back", partial(join_back_kernel, len(parts)), 1, ins, outs, 10**6, 16)

    kept = []
    for l in range(layers):
        weights = [key_weight, value_weight, query_weight, output_weight]
        own, sib, *saved = run(
            "attend",
            partial(attend_kernel, n),
            images,
            [image(a) for a in x_all]
            + route_sets(0, l)
            + [(w, at_layer(l), "hbm") for w in weights],
            [partial_rows, partial_rows, all_rows, slot_rows, slot_rows, all_rows, all_rows]
            + [(probs_shape, bf16, per_image, "hbm"), slot_rows, slot_rows, gate_rows],
            2 * flop_core + 6 * flop_small,
            32,
            [pltpu.VMEM((features, total), bf16), pltpu.VMEM((features, slots), f32)],
        )
        low_a = low
        middle, low = join(
            scatter(own, sib), state, perceptron_gain[l : l + 1], perceptron_shift[l : l + 1]
        )
        x_all = gather(low)
        ff_weights = [up_weight, down_weight]
        route_ins = route_sets(1, l)
        last = l == layers - 1
        if last:
            for j in copies_all:
                x_all[-1], copies_all[j] = lax.optimization_barrier((x_all[-1], copies_all[j]))
        own, sib, copies, slope, result, gate, *active = run(
            "perceptron",
            partial(perceptron_kernel, n, chunk),
            images,
            [image(a) for a in x_all] + route_ins + [(w, at_layer(l), "hbm") for w in ff_weights],
            [partial_rows, partial_rows, slot_rows, wide_rows, slot_rows, gate_rows] + wide_kept,
            2 * flop_wide,
            32,
        )
        kept_ff = (copies, slope, result, gate)
        if few:
            copies_all[l] = lax.all_gather(copies, "dp", axis=0, tiled=False)
        parts = scatter(own, sib)
        if last:
            (after,) = join(parts, middle, None, None)
            low_next = None
        else:
            after, low_next = join(
                parts, middle, attention_gain[l + 1 : l + 2], attention_shift[l + 1 : l + 2]
            )
        kept.append((state, low_a, saved, middle, low, copies, active, kept_ff, after))
        state = after
        low = low_next
        if not last:
            x_all = gather(low)

    grad = cotangent.astype(f32)
    grad_low = None
    gains, columns, shares, ff_parts, qo_parts = [], [], [], [], []
    steps = hidden // width
    halves = ((0, steps // 2), (steps // 2, steps - steps // 2))
    waiting = [(l, *half) for l in range(layers) for half in halves[::-1]] if few else []
    written, experts = [()], []

    def ff_step(arrived, times=2, last=False):
        for l, start, count in [waiting.pop() for _ in range(times) if waiting]:
            written[0] = ff_gradient(
                [copies_all[l], gr_all[l]],
                up_weight,
                down_weight,
                l,
                width,
                start,
                count,
                written[0],
            )
        if few:
            due = experts if last else []
            arrived[-1], written[0], experts[: len(due)] = lax.optimization_barrier(
                (arrived[-1], written[0], due)
            )
    for l in range(layers - 1, -1, -1):
        state, low_a, saved, middle, low_m, copies, active, kept_ff, after = kept[l]
        ff_weights = [up_weight, down_weight]
        last = l == layers - 1
        g_all = cotangent_all if last else [image(a) for a in gather(grad_low)]
        outs = run(
            "perceptron_back",
            partial(perceptron_back_kernel, n, rows, chunk),
            images,
            g_all
            + route_sets(1, l)[1:]
            + [(w, at_layer(l), "hbm") for w in ff_weights]
            + [(a, per_image, "hbm") for a in kept_ff],
            [router_rows] * (not last)
            + [partial_rows, partial_rows, slot_rows, router_rows]
            + wide_kept,
            2 * flop_wide,
            32,
        )
        if not last:
            columns[-1] = columns[-1] + outs[0]
            outs = outs[1:]
        own, sib, gr, router_m, *gh = outs
        parts = scatter(own, sib)
        if few:
            gr_all[l] = lax.all_gather(gr, "dp", axis=0, tiled=False)
            if not last:
                parts[-1], copies_all[l + 1], gr_all[l + 1] = lax.optimization_barrier(
                    (parts[-1], copies_all[l + 1], gr_all[l + 1])
                )
        else:
            up_part = jnp.einsum("isd,isf->df", copies, gh[0], preferred_element_type=f32)
            down_part = jnp.einsum("isf,isd->fd", active[0], gr, preferred_element_type=f32)
            both = (up_part.astype(bf16), down_part.astype(bf16))
            ff_parts.append(lax.psum(both, "dp"))
        grad, grad_low, gain_m, shift_m, _ = join_back(
            parts,
            grad,
            middle,
            after,
            low_m,
            1,
            l,
            perceptron_gain[l : l + 1],
        )
        columns.append(router_m)
        g_all = gather(grad_low)
        x, copies, queries, keys, values, probs, mixed, result, gate = saved
        weights = [key_weight, value_weight, query_weight, output_weight]
        own, sib, gr_a, dq, router_a, home = run(
            "attend_back",
            partial(attend_back_kernel, n, rows),
            images,
            [image(a) for a in g_all]
            + [(me[None], in_smem)]
            + route_sets(0, l)[1:]
            + [(w, at_layer(l), "hbm") for w in weights]
            + [(a, per_image, "hbm") for a in saved],
            [(back_shape, bf16, whole), (back_shape, bf16, whole)]
            + [slot_rows, slot_rows, router_rows, router_rows],
            4 * flop_core + 14 * flop_small,
            32,
            [pltpu.VMEM((features, features), f32)] * 2
            + [
                pltpu.VMEM((slots, features), bf16),
                pltpu.VMEM((features, total), bf16),
                pltpu.VMEM((features, slots), f32),
                pltpu.VMEM((total, features), bf16),
                pltpu.VMEM((total, features), bf16),
            ],
        )
        columns[-1] = columns[-1] + home
        columns.append(router_a)
        later = [gr_all[layers - 1]] if few and l == 0 < layers - 1 else []
        parts = scatter(own, sib, later)
        if later:
            gr_all[layers - 1] = later[0]
        both = (
            jnp.einsum("isd,isf->df", copies, dq, preferred_element_type=f32).astype(bf16),
            jnp.einsum("isf,isd->fd", mixed, gr_a, preferred_element_type=f32).astype(bf16),
        )
        parts[-1], *both = lax.optimization_barrier((parts[-1], *both))
        qo_parts.append(both)
        if few and l < layers - 1:
            parts[-1], gr_all[l] = lax.optimization_barrier((parts[-1], gr_all[l]))
            if l == 0:
                ff_step(parts, 1)
        grad, grad_low, gain_a, shift_a, late, share = join_back(
            parts,
            grad,
            state,
            middle,
            low_a,
            0,
            l,
            attention_gain[l : l + 1],
        )
        gains.append((gain_a, shift_a, gain_m, shift_m))
        shares.append(share)

    if few:
        qo_parts, gr_all[0] = lax.optimization_barrier((qo_parts, gr_all[0]))

    experts += list(zip(*lax.psum(qo_parts, "dp")))
    picked = (task_index[:, None] == jnp.arange(tasks, dtype=jnp.int32)[None, :]).astype(f32)
    highest = lax.Precision.HIGHEST
    columns = jnp.stack([c[:, 0] for c in columns[::-1]])
    columns = jnp.einsum("it,lid->ltd", picked, columns, precision=highest)
    late = jnp.einsum("it,ied->ted", picked, late, precision=highest)
    vectors = [v for items in gains[::-1] for v in items]
    payload = [
        *shares[::-1],
        late.reshape(tasks * n, features).astype(bf16),
        *[v.astype(bf16) for v in vectors],
        columns.reshape(layers * 2 * tasks, features).astype(bf16),
    ]
    used = sum(p.shape[0] for p in payload)
    payload.append(jnp.zeros((-used % 16, features), bf16))
    shared = dp_add(jnp.concatenate(payload, axis=0), ff_step)

    def end(arrived):
        ff_step(arrived, len(waiting), True)

    found = gather(shared, end)
    if few:
        experts = [*widen([items[::-1] for items in experts]), *written[0]]
    else:
        experts = [jnp.stack(items[::-1]).astype(f32)[:, None] for items in experts]
        experts += [jnp.stack(items[::-1]).astype(f32)[:, None] for items in zip(*ff_parts)]
    matrix = ((layers, features, features), f32, whole)
    keys, values, columns, vectors, late = run(
        "assemble",
        partial(assemble_kernel, n, layers, tasks),
        1,
        [(me[None], in_smem)] + [const(a) for a in found],
        [
            matrix,
            matrix,
            ((n, layers * 2 * tasks, features), f32, whole),
            ((len(vectors), features), f32, whole),
            ((tasks * n, features), f32, whole),
        ],
        0,
        24,
    )
    columns = columns.reshape(n, layers, 2, tasks, features).transpose(2, 1, 3, 4, 0)
    late = late.reshape(tasks, n, features).transpose(0, 2, 1)
    attention_columns = jnp.concatenate([columns[0, :1] + late, columns[0, 1:]], axis=0)
    vectors = vectors.reshape(layers, 4, features).transpose(1, 0, 2)
    return (
        kept[-1][-1],
        grad,
        *(vectors[j] for j in range(4)),
        keys,
        values,
        *experts,
        attention_columns,
        columns[1],
    )


def solution(mesh):
    in_specs = (
        P("dp", "expert", None),
        P(None, "dp", "expert", None),
        P(None, "dp", "expert", None),
        P("dp"),
        P(),
        P(),
        P(),
        P(),
        P(),
        P(),
        P(None, "expert", None, None),
        P(None, "expert", None, None),
        P(None, "expert", None, None),
        P(None, "expert", None, None),
        P(),
        P(),
        P("dp", "expert", None),
    )
    out_specs = (
        P("dp", "expert", None),
        P("dp", "expert", None),
        P(),
        P(),
        P(),
        P(),
        P(),
        P(),
        P(None, "expert", None, None),
        P(None, "expert", None, None),
        P(None, "expert", None, None),
        P(None, "expert", None, None),
        P(),
        P(),
    )
    return jax.shard_map(local, mesh=mesh, in_specs=in_specs, out_specs=out_specs, check_vma=False)
```
